32 devices in a mesh: rep: 8 (over y, x, core), fsdp: 4 (over z).
Axes of the slice: x: 2, y: 2, z: 4, core: 2. Of those that a mesh axis runs over, the one named last changes fastest.
Arguments:
- tokens: bfloat16 [8, 1024, 2048], P('rep', 'fsdp'), may hold values from -6 to 6
- cotangent: bfloat16 [8, 1024, 2048], P('rep', 'fsdp'), may hold values from -6 to 6
- lengths: int32 [8], P('rep'), may hold values from 256 to 1024, as said below
- w_mix: float32 [4, 2048, 2048], P(None, 'fsdp', 'rep'), may hold values from -0.125 to 0.125
- w_in: float32 [2, 2048, 5632], P(None, 'fsdp', 'rep'), may hold values from -0.125 to 0.125
- w_down: float32 [5632, 2048], P('fsdp', 'rep'), may hold values from -0.078125 to 0.078125
- gains: float32 [4, 2048], P(None, 'fsdp')
- m_mix: float32 [4, 2048, 2048], P(None, 'fsdp', 'rep'), may hold values from -224 to 224
- m_in: float32 [2, 2048, 5632], P(None, 'fsdp', 'rep'), may hold values from -224 to 224
- m_down: float32 [5632, 2048], P('fsdp', 'rep'), may hold values from -224 to 224
- m_gain: float32 [4, 2048], P(None, 'fsdp'), may hold values from -224 to 224
- v_mix: float32 [4, 2048, 2048], P(None, 'fsdp', 'rep'), may hold values from 819.2 to 3276.8
- v_in: float32 [2, 2048, 5632], P(None, 'fsdp', 'rep'), may hold values from 819.2 to 3276.8
- v_down: float32 [5632, 2048], P('fsdp', 'rep'), may hold values from 819.2 to 3276.8
- v_gain: float32 [4, 2048], P(None, 'fsdp'), may hold values from 819.2 to 3276.8
Outputs:
- mixed: bfloat16 [8, 1024, 2048], P('rep', 'fsdp')
- token_grad: float32 [8, 1024, 2048], P('rep', 'fsdp')
- new_mix: float32 [4, 2048, 2048], P(None, 'fsdp', 'rep')
- new_in: float32 [2, 2048, 5632], P(None, 'fsdp', 'rep')
- new_down: float32 [5632, 2048], P('fsdp', 'rep')
- new_gains: float32 [4, 2048], P(None, 'fsdp')
- first_mix: float32 [4, 2048, 2048], P(None, 'fsdp', 'rep')
- first_in: float32 [2, 2048, 5632], P(None, 'fsdp', 'rep')
- first_down: float32 [5632, 2048], P('fsdp', 'rep')
- first_gains: float32 [4, 2048], P(None, 'fsdp')
- second_mix: float32 [4, 2048, 2048], P(None, 'fsdp', 'rep')
- second_in: float32 [2, 2048, 5632], P(None, 'fsdp', 'rep')
- second_down: float32 [5632, 2048], P('fsdp', 'rep')
- second_gains: float32 [4, 2048], P(None, 'fsdp')
- copy_mix: bfloat16 [4, 2048, 2048], P(None, 'fsdp', 'rep')
- copy_in: bfloat16 [2, 2048, 5632], P(None, 'fsdp', 'rep')
- copy_down: bfloat16 [5632, 2048], P('fsdp', 'rep')
The draws below stay inside these ranges and needn't reach their ends.
Inputs may be any that keep to these rules, and one draw needn't show every extreme that they name: `lengths`: every length lies between 256 and 1024; at least one sequence has length 1024.
All inputs are finite; a program needn't handle non-finite values.
Results may differ from the reference program's by a relative error of at most 0.0085.
The reference program's roundings to bfloat16 on the way (of `weights`) count: a program that leaves them out, or rounds other values in their place, can miss the bound.
Values may be sent and summed in bfloat16 or wider, within the bound.
No kernel may reach another device: no remote copies, remote signals or barrier semaphores. Data moves between devices by JAX's collectives and lax.ppermute only.
A program may use at most 640 MiB of HBM per device.

```python
import math
import jax
import jax.numpy as jnp
from jax import lax

D = 2048
FF = 5632
HEAD = 128
STRETCH = 32
STEP = 10
SEQ_LEN = 1024
SEQS = 8


def draw_lengths(key, part):
    key = jax.random.fold_in(key, 11)
    first_key, second_key = jax.random.split(key)
    base = jax.random.randint(first_key, (SEQS,), SEQ_LEN // 4, SEQ_LEN + 1)
    chosen = jax.random.randint(second_key, (), 0, SEQS)
    return jnp.where(jnp.arange(SEQS) == chosen, SEQ_LEN, base).astype(jnp.int32)


def draw_gains(key, part):
    key = jax.random.fold_in(key, 5)
    first_key, second_key = jax.random.split(key)
    ramp = 0.5 + jnp.arange(D, dtype=jnp.float32) / D
    spread = jax.random.uniform(first_key, (3, D), jnp.float32, 0.8, 1.25)
    forget_bias = jax.random.uniform(second_key, (1, D), jnp.float32, 2.5, 8.0)
    return jnp.concatenate([ramp[None] * spread, forget_bias], axis=0).astype(jnp.float32)


def block_levels(rng, dims, cuts, smallest, largest):
    def one(axis_at, blocks):
        steps = jax.random.uniform(jax.random.fold_in(jax.random.fold_in(rng, 6), axis_at), (blocks,), jnp.float32, smallest / len(cuts), largest / len(cuts))
        return jnp.repeat(jnp.exp(steps), dims[axis_at] // blocks).reshape((-1,) + (1,) * (len(dims) - axis_at - 1))

    level = one(*cuts[0])
    for cut in cuts[1:]:
        level = level * one(*cut)
    return level


def normal_values(own_key, extent, width, reach, cuts=(), held_as=jnp.bfloat16):
    result = jax.random.normal(own_key, extent, jnp.float32) * width
    if len(cuts) > 0:
        result = block_levels(own_key, extent, cuts, -0.22, 0.18) * result
    return jnp.clip(result, min=-reach, max=reach).astype(held_as)


def setup_inputs(seed: int = 0) -> dict:
    splits = jax.random.split(jax.random.key(seed), 16)
    return {
        "tokens": normal_values(splits[0], (SEQS, SEQ_LEN, D), 1.0, 6.0, ((0, 8), (1, 4))),
        "cotangent": normal_values(splits[1], (SEQS, SEQ_LEN, D), 1.0, 6.0, ((0, 8), (1, 4))),
        "lengths": draw_lengths(jax.random.fold_in(splits[15], 71), 0),
        "w_mix": normal_values(splits[3], (4, D, D), D ** -0.5, 0.125, ((1, 4), (2, 8)), jnp.float32),
        "w_in": normal_values(splits[4], (2, D, FF), D ** -0.5, 0.125, ((1, 4), (2, 8)), jnp.float32),
        "w_down": normal_values(splits[5], (FF, D), FF ** -0.5, 0.078125, ((0, 4), (1, 8)), jnp.float32),
        "gains": draw_gains(jax.random.fold_in(splits[15], 71), 0),
        "m_mix": normal_values(splits[7], (4, D, D), (0.4 * (SEQS * SEQ_LEN) ** 0.5), 224.0, ((1, 4), (2, 8)), jnp.float32),
        "m_in": normal_values(splits[8], (2, D, FF), (0.4 * (SEQS * SEQ_LEN) ** 0.5), 224.0, ((1, 4), (2, 8)), jnp.float32),
        "m_down": normal_values(splits[9], (FF, D), (0.4 * (SEQS * SEQ_LEN) ** 0.5), 224.0, ((0, 4), (1, 8)), jnp.float32),
        "m_gain": normal_values(splits[10], (4, D), (0.4 * (SEQS * SEQ_LEN) ** 0.5), 224.0, ((1, 4),), jnp.float32),
        "v_mix": jnp.clip(jnp.exp(math.log(3276.8) - 1.3862944 * jax.random.uniform(splits[11], (4, D, D), jnp.float32) ** block_levels(splits[11], (4, D, D), ((1, 4), (2, 8)), -0.2, 0.2)), 819.2, 3276.8),
        "v_in": jnp.clip(jnp.exp(math.log(3276.8) - 1.3862944 * jax.random.uniform(splits[12], (2, D, FF), jnp.float32) ** block_levels(splits[12], (2, D, FF), ((1, 4), (2, 8)), -0.2, 0.2)), 819.2, 3276.8),
        "v_down": jnp.clip(jnp.exp(math.log(3276.8) - 1.3862944 * jax.random.uniform(splits[13], (FF, D), jnp.float32) ** block_levels(splits[13], (FF, D), ((0, 4), (1, 8)), -0.2, 0.2)), 819.2, 3276.8),
        "v_gain": jnp.clip(jnp.exp(math.log(3276.8) - 1.3862944 * jax.random.uniform(splits[14], (4, D), jnp.float32) ** block_levels(splits[14], (4, D), ((1, 4),), -0.2, 0.2)), 819.2, 3276.8),
    }


@jax.custom_vjp
def low(v):
    return lax.optimization_barrier(v.astype(jnp.bfloat16)).astype(jnp.float32)

@jax.custom_vjp
def low_back(v):
    return v

def low_keep(v):
    return (low(v), None)

def low_pass(kept, grad):
    return (grad,)

def back_keep(v):
    return (v, None)

def back_low(kept, grad):
    return (low(grad),)
low.defvjp(low_keep, low_pass)
low_back.defvjp(back_keep, back_low)
epsilon = 1e-06
adam_epsilon = 1e-08
beta_first = 0.5
beta_second = 0.5
rate_matrix = 0.04
rate_gain = 0.3
decay_matrix = 0.1
highest_precision = lax.Precision.HIGHEST

def rms_scale(value_input, scales):
    return value_input * lax.rsqrt(lax.optimization_barrier(jnp.mean(value_input * value_input, axis=-1, keepdims=True)) + epsilon) * scales

def gate_terms(query_pre, forget_pre, forget_bias):
    shifted = forget_pre + forget_bias
    return (jax.nn.silu(query_pre), jax.nn.log_sigmoid(shifted), jax.nn.sigmoid(-shifted))

def stretch_step(initial_state, block_data):
    query_input, log_decay, input_keys, value_input = block_data
    cumulative_decay = jnp.cumsum(log_decay, axis=0)
    block_len = query_input.shape[0]
    causal = (jnp.arange(block_len)[:, None] >= jnp.arange(block_len)[None, :])[:, :, None, None]
    log_gap = jnp.where(causal, cumulative_decay[:, None] - cumulative_decay[None, :], 0.0)
    weights = jnp.where(causal, jnp.exp(log_gap), 0.0)
    scores = jnp.einsum('thk,tshk,shk->tsh', query_input, weights, input_keys, precision=highest_precision)
    inside = jnp.einsum('tsh,shv->thv', scores, value_input, precision=highest_precision)
    outside_state = jnp.einsum('nip,ipc->nic', query_input * jnp.exp(cumulative_decay), initial_state, precision=highest_precision)
    final_log_decay = cumulative_decay[-1]
    carried_state = jnp.exp(final_log_decay)[:, :, None] * initial_state + jnp.einsum('ril,rit->ilt', input_keys * jnp.exp(final_log_decay[None] - cumulative_decay), value_input, precision=highest_precision)
    return (carried_state, inside + outside_state)

def recurrence(query_input, log_decay, input_keys, value_input, initial_state):
    row_count = query_input.shape[0]

    def blocked(source):
        return source.reshape((row_count // STRETCH, STRETCH) + source.shape[1:])
    end_state, outputs = lax.scan(jax.checkpoint(stretch_step), initial_state, (blocked(query_input), blocked(log_decay), blocked(input_keys), blocked(value_input)))
    return (outputs.reshape((row_count,) + outputs.shape[2:]), end_state)

def matmul(left, right):
    return jnp.dot(left, right, precision=highest_precision)

def layer(params, inputs):
    w_mix, w_in, w_down, gains = params
    mixing = low(w_mix)
    feeding = low(w_in)
    project_down = low(w_down)
    scales = low(gains)
    head_count = D // HEAD
    row_count = inputs.shape[0]
    normed_a = low(rms_scale(inputs, scales[0]))
    query_pre = low_back(matmul(normed_a, mixing[0]))
    forget_pre = low_back(matmul(normed_a, mixing[1]))
    value_pre = low_back(matmul(normed_a, mixing[2]))
    act_query, log_decay, input_keys = gate_terms(query_pre, forget_pre, scales[3])

    def heads_of(source):
        return source.reshape(row_count, head_count, HEAD)
    outputs, end_state = recurrence(heads_of(act_query), heads_of(log_decay), heads_of(input_keys), heads_of(value_pre), jnp.zeros((head_count, HEAD, HEAD), jnp.float32))
    head_out = low(rms_scale(outputs, scales[2].reshape(head_count, HEAD)).reshape(row_count, D))
    middle = inputs + low_back(matmul(head_out, mixing[3]))
    normed_b = low(rms_scale(middle, scales[1]))
    gate_pre = low_back(matmul(normed_b, feeding[0]))
    up_pre = low_back(matmul(normed_b, feeding[1]))
    hidden = low(jax.nn.silu(gate_pre) * up_pre)
    return middle + low_back(matmul(hidden, project_down))

def adam(weight, first, second, gradient, step_rate, decay_on):
    first_new = beta_first * first + (1.0 - beta_first) * gradient
    second_new = beta_second * second + (1.0 - beta_second) * gradient * gradient
    first_fix = 1.0 - beta_first ** STEP
    second_fix = 1.0 - beta_second ** STEP
    weight_new = weight - step_rate * (first_new / first_fix / (jnp.sqrt(second_new / second_fix) + adam_epsilon) + decay_on * weight)
    return (weight_new, first_new, second_new)

def reference(tokens, cotangent, lengths, w_mix, w_in, w_down, gains, m_mix, m_in, m_down, m_gain, v_mix, v_in, v_down, v_gain):
    params = (w_mix, w_in, w_down, gains)
    position = jnp.arange(SEQ_LEN).astype(jnp.int32)

    def per_sequence(total_grads, sequence_item):
        sequence, cot_seq, length = sequence_item
        layer_out, pull_back = jax.vjp(layer, params, sequence.astype(jnp.float32))
        valid = (position < length).astype(jnp.float32)[:, None]
        weight_grads, input_grad = pull_back(cot_seq.astype(jnp.float32) * valid)
        total_grads = jax.tree.map(jnp.add, total_grads, weight_grads)
        return (total_grads, (layer_out.astype(jnp.bfloat16), input_grad))
    start_grads = jax.tree.map(jnp.zeros_like, params)
    grads_all, (mixed, token_grad) = lax.scan(per_sequence, start_grads, (tokens, cotangent, lengths))
    grad_mix, grad_in, grad_down, grad_gain = grads_all
    new_mix, first_mix, second_mix = adam(w_mix, m_mix, v_mix, grad_mix, rate_matrix, decay_matrix)
    new_in, first_in, second_in = adam(w_in, m_in, v_in, grad_in, rate_matrix, decay_matrix)
    new_down, first_down, second_down = adam(w_down, m_down, v_down, grad_down, rate_matrix, decay_matrix)
    new_gains, first_gains, second_gains = adam(gains, m_gain, v_gain, grad_gain, rate_gain, 0.0)
    return (mixed, token_grad, new_mix, new_in, new_down, new_gains, first_mix, first_in, first_down, first_gains, second_mix, second_in, second_down, second_gains, new_mix.astype(jnp.bfloat16), new_in.astype(jnp.bfloat16), new_down.astype(jnp.bfloat16))
```

```python
import functools
import math

import jax
import jax.numpy as jnp
import numpy as np
from jax import lax
from jax.experimental import pallas as pl
from jax.experimental.pallas import tpu as pltpu
from jax.sharding import PartitionSpec as P

D = 2048
HEAD = 128
STEP = 10
PACK = HEAD + 32

epsilon = 1e-06
adam_epsilon = 1e-08
beta_first = 0.5
beta_second = 0.5
rate_matrix = 0.04
rate_gain = 0.3
decay_matrix = 0.1
bf16 = jnp.bfloat16
f32 = jnp.float32


def swap(x, axis, d):
    n = lax.axis_size(axis)
    return lax.ppermute(x, axis, [(i, i ^ d) for i in range(n)])


def block_of(x, index):
    return lax.dynamic_index_in_dim(x, index, 0, False)


def low_bit(j):
    return j & -j


def z_pieces(x, *lands):
    n = lax.axis_size("fsdp")
    pieces, landed = {0: x}, ()
    for hop in range(1, n.bit_length()):
        now = [j for j in range(n) if j.bit_count() == hop]
        got = {j: swap(after(pieces[j & (j - 1)], *landed), "fsdp", low_bit(j)) for j in now}
        if hop <= len(lands):
            got = {j: after(piece, *lands[hop - 1]) for j, piece in got.items()}
        pieces.update(got)
        landed = tuple(got.values())
    return [pieces[j] for j in range(n)]


def kernel_call(body, grid, in_specs, out_specs, out_shape, name, us, prefetch=(), aliases=None):
    return pl.pallas_call(
        body,
        grid_spec=pltpu.PrefetchScalarGridSpec(
            num_scalar_prefetch=len(prefetch), grid=grid, in_specs=in_specs, out_specs=out_specs
        ),
        out_shape=out_shape,
        name=name,
        input_output_aliases=aliases or {},
        cost_estimate=pl.CostEstimate(flops=0, bytes_accessed=int(us * 5e4), transcendentals=0),
        compiler_params=pltpu.CompilerParams(
            dimension_semantics=("arbitrary",) * len(grid), vmem_limit_bytes=52 * 1024 * 1024
        ),
    )


def whole_spec(x, buffers=2):
    return pl.BlockSpec(x.shape, lambda *_: (0,) * x.ndim, pipeline_mode=pl.Buffered(buffers))


def layer_spec(x, at):
    return pl.BlockSpec((None,) + x.shape[1:], lambda *_: (at, 0, 0), pipeline_mode=pl.Buffered(1))


def index_of(axis):
    return lax.axis_index(axis).astype(jnp.int32).reshape(1)


class ZReduce:
    def __init__(self, sums):
        self.sums = list(sums)
        self.left = list(range(len(self.sums) - 1, 0, -1))
        self.flying = []
        self.send()

    def send(self, *others):
        most = max(j.bit_count() for j in self.left)
        now = [j for j in self.left if j.bit_count() == most]
        self.left = [j for j in self.left if j.bit_count() < most]
        self.sent = [after(self.sums[j].astype(bf16), *others) for j in now]
        self.flying += [(j, swap(x, "fsdp", low_bit(j))) for j, x in zip(now, self.sent)]

    def advance(self, *others):
        first = not self.left
        landed, self.flying = self.flying, []
        self.landed = [got for _, got in landed]
        for j, got in landed:
            got = after(got, *others)
            self.sums[j & (j - 1)] = self.sums[j & (j - 1)].astype(f32) + got.astype(f32)
        if not first:
            self.send(*self.landed, *others)
        return self.sums[0]

    def flying_now(self):
        return [got for _, got in self.flying]

    def finish(self, *others):
        while self.flying:
            total = self.advance(*others)
        return total


def after(x, *others):
    return lax.optimization_barrier((x,) + others)[0]


def chip_masks():
    masks = []
    while 2 << len(masks) < lax.axis_size("rep"):
        masks.append(2 << len(masks))
    return masks


def rep_gather(x, sends=(), lands=(), before_far=()):
    rows = x.shape[0] // 2
    masks = chip_masks()
    upper, lower = x[None, :rows], x[None, rows:]
    for step in range(len(masks)):
        if step < len(sends):
            upper, lower = after(upper, *sends[step]), after(lower, *sends[step])
        got = swap(upper, "rep", masks[step])
        other = swap(lower, "rep", masks[-1 - step])
        got, other = lax.optimization_barrier((got, other) + tuple(lands[step] if step < len(lands) else ()))[:2]
        upper = jnp.concatenate([upper, got])
        lower = jnp.stack([lower, other], axis=1).reshape((2 * lower.shape[0],) + lower.shape[1:])
    near = after(jnp.stack([upper, lower]), *before_far)
    return near, swap(near, "rep", 1)


class RepReduce:
    def __init__(self, far):
        self.got = swap(far, "rep", 1)
        self.masks = chip_masks()

    def begin(self, send_upper, send_lower, keep_upper, keep_lower):
        self.upper, self.lower = keep_upper, keep_lower
        self.sent = (send_upper, send_lower)
        self.fly(0)

    def fly(self, step):
        self.flying = (
            swap(self.sent[0], "rep", self.masks[-1 - step]),
            swap(self.sent[1], "rep", self.masks[step]),
        )

    def advance(self, *others):
        self.landed = self.flying
        upper, lower = lax.optimization_barrier(tuple(self.flying) + others)[:2]
        self.flying = None
        if self.upper.shape[0] == 1:
            self.last = (upper[0], lower[0])
            return
        half = self.upper.shape[0] // 2
        *sent, self.upper, self.lower = step_sums(self.upper, upper, self.lower, lower)
        self.sent = sent
        self.fly(len(self.masks) - half.bit_length())

    def finish(self, *others):
        while self.flying is not None:
            self.advance(*others)
        return self.upper[0], self.lower[0], *self.last


def step_kernel(keep_upper_ref, got_upper_ref, keep_lower_ref, got_lower_ref, *outs):
    half = keep_upper_ref.shape[0] // 2
    for i in range(half):
        upper = keep_upper_ref[i] + got_upper_ref[i].astype(f32)
        outs[2][i] = upper
        outs[0][i] = (keep_upper_ref[half + i] + got_upper_ref[half + i].astype(f32)).astype(bf16)
        outs[3][i] = keep_lower_ref[2 * i] + got_lower_ref[2 * i].astype(f32)
        outs[1][i] = (keep_lower_ref[2 * i + 1] + got_lower_ref[2 * i + 1].astype(f32)).astype(bf16)


def step_sums(keep_upper, got_upper, keep_lower, got_lower):
    count, rows, d = keep_upper.shape
    block = 32
    whole = pl.BlockSpec((count, block, d), lambda i: (0, i, 0))
    half = pl.BlockSpec((count // 2, block, d), lambda i: (0, i, 0))
    shape = (count // 2, rows, d)
    return kernel_call(
        step_kernel,
        (rows // block,),
        [whole] * 4,
        [half] * 4,
        [jax.ShapeDtypeStruct(shape, bf16)] * 2 + [jax.ShapeDtypeStruct(shape, f32)] * 2,
        "step_sums",
        3,
    )(keep_upper, got_upper, keep_lower, got_lower)


def place_kernel(me_ref, near_ref, far_ref, out_ref):
    rows = near_ref.shape[2]
    near = pl.program_id(0) < pl.num_programs(0) // 2
    out_ref[:rows] = jnp.where(near, near_ref[0, 0], far_ref[0, 0])
    out_ref[rows:] = jnp.where(near, near_ref[1, 0], far_ref[1, 0])


def place_columns(near, far):
    _, chips, rows, width = near.shape
    return kernel_call(
        place_kernel,
        (2 * chips,),
        [
            pl.BlockSpec((2, 1, rows, width), lambda p, me: (0, jnp.minimum(p, chips - 1), 0, 0)),
            pl.BlockSpec((2, 1, rows, width), lambda p, me: (0, jnp.maximum(p - chips, 0), 0, 0)),
        ],
        pl.BlockSpec((2 * rows, width), lambda p, me: (0, me[0] ^ (2 * lax.rem(p, chips) + p // chips))),
        jax.ShapeDtypeStruct((2 * rows, 2 * chips * width), near.dtype),
        "place_columns",
        7,
        (index_of("rep"),),
    )(index_of("rep"), near, far)


def rep_exchange(x):
    return lax.all_to_all(x, "rep", 0, 0)


def all_sum(x, axis):
    d = 1
    while d < lax.axis_size(axis):
        x = x + swap(x, axis, d)
        d *= 2
    return x


def split(x):
    high = x.astype(bf16)
    return high, (x - high.astype(f32)).astype(bf16)


def dot3(a, b, ca, cb):
    left = jnp.concatenate([a[0], a[0], a[1]], axis=ca)
    right = jnp.concatenate([b[0], b[1], b[0]], axis=cb)
    return lax.dot_general(left, right, (((ca,), (cb,)), ((), ())), preferred_element_type=f32)


def dot3_wide(a, b):
    both = jnp.dot(a[0], jnp.concatenate(b, axis=1), preferred_element_type=f32)
    return both[:, :HEAD] + both[:, HEAD:] + jnp.dot(a[1], b[0], preferred_element_type=f32)


def range_sums(matrix, x):
    width = x.shape[1]
    both = jnp.dot(matrix, jnp.concatenate(split(x), axis=1), preferred_element_type=f32)
    return both[:, :width] + both[:, width:]


def log_decay_of(z):
    return jnp.minimum(z, 0.0) - jnp.log1p(jnp.exp(-jnp.abs(z)))


def head_slice(h):
    return slice(h * HEAD, (h + 1) * HEAD)


def pack_store(ref, h, state, decay):
    ref[0, h, :HEAD, :] = state.astype(bf16)
    high, low = split(jnp.broadcast_to(decay, (16, HEAD)))
    ref[0, h, HEAD : HEAD + 16, :] = high
    ref[0, h, HEAD + 16 :, :] = low


def entry_kernel(me_ref, after_ref, x_ref, *refs):
    *pieces, scale_ref, a_ref, qfi_ref, weight_ref, last_ref, state_ref, out_ref, fb_ref = refs
    rows, wide = pieces[0].shape[0] - 16, weight_ref.shape[1]
    width = fb_ref.shape[1]

    @pl.when(pl.program_id(0) == 0)
    def _():
        for j, piece in enumerate(pieces):
            at = pl.ds(pl.multiple_of((me_ref[0] ^ j) * rows, rows), rows)
            weight_ref[at, :] = piece[:rows, :wide]
            last_ref[at, :] = piece[:rows, wide:]
            scale_ref[:, at] = piece[rows:, :rows].astype(f32)
        fb_ref[...] = scale_ref[3:4, pl.ds(pl.multiple_of(me_ref[1] * width, width), width)]

    x = x_ref[...].astype(f32)
    size = lax.rsqrt(jnp.mean(x * x, axis=1, keepdims=True) + epsilon)
    a_ref[...] = (x * size * scale_ref[0:1, :]).astype(bf16)
    qfi_ref[...] = jnp.dot(a_ref[...], weight_ref[...], preferred_element_type=f32)
    z = qfi_ref[:, width : 2 * width] + fb_ref[...]
    log_decay = log_decay_of(z)
    to_end = range_sums(after_ref[...], log_decay)
    keys = jax.nn.sigmoid(-z) * jnp.exp(to_end)
    decay = jnp.exp(jnp.sum(log_decay, axis=0, keepdims=True))
    for h in range(width // HEAD):
        at = head_slice(h)
        value = qfi_ref[:, 2 * width + h * HEAD : 2 * width + (h + 1) * HEAD]
        state = dot3(split(value), split(keys[:, at]), 0, 0)
        state_ref[0, h] = state
        pack_store(out_ref, h, state, decay[:, at])


def level_masks(size):
    row = lax.broadcasted_iota(jnp.int32, (size, size), 0)
    col = lax.broadcasted_iota(jnp.int32, (size, size), 1)
    return row, col, row ^ col


def inside_kernel(levels_ref, fb_ref, q_ref, f_ref, i_ref, *refs):
    out_ref, high_ref, low_ref = refs[-3:]
    size = q_ref.shape[0]
    count = levels_ref.shape[0] // size
    z = f_ref[...] + fb_ref[...]
    weights = jnp.exp(range_sums(levels_ref[...], log_decay_of(z)))
    keys = jax.nn.sigmoid(-z)
    q = q_ref[...]
    query = q * jax.nn.sigmoid(q)
    row, col, differ = level_masks(size)
    later = row > col
    for h in range(q_ref.shape[1] // HEAD):
        at = head_slice(h)
        hq, hk = query[:, at], keys[:, at]
        scores = jnp.where(row == col, jnp.sum(hq * hk, axis=1, keepdims=True), 0.0)
        for l in range(count):
            w = weights[l * size : (l + 1) * size, at]
            part = dot3(split(hq * w), split(hk * w), 1, 1)
            scores = jnp.where(later & ((differ >> l) == 1), part, scores)
        high, low = split(scores)
        high_ref[0, h] = high
        low_ref[0, h] = low
        out_ref[:, at] = dot3((high, low), split(i_ref[:, at]), 1, 0)


def output_kernel(upto_ref, fb_ref, scale_ref, q_ref, f_ref, inside_ref, state_ref, out_ref, u_ref):
    q = q_ref[...]
    reach = q * jax.nn.sigmoid(q) * jnp.exp(range_sums(upto_ref[...], log_decay_of(f_ref[...] + fb_ref[...])))
    for h in range(q_ref.shape[1] // HEAD):
        at = head_slice(h)
        o = inside_ref[:, at] + dot3(split(reach[:, at]), split(state_ref[0, h]), 1, 1)
        out_ref[:, at] = o
        size = lax.rsqrt(jnp.mean(o * o, axis=1, keepdims=True) + epsilon)
        u_ref[:, at] = (o * size * scale_ref[:, at]).astype(bf16)


def back_state_kernel(upto_ref, fb_ref, scale_ref, q_ref, f_ref, o_ref, du_ref, do_ref, out_ref, dscale_ref):
    @pl.when(pl.program_id(0) == 0)
    def _():
        dscale_ref[...] = jnp.zeros_like(dscale_ref)

    q = q_ref[...]
    log_decay = log_decay_of(f_ref[...] + fb_ref[...])
    reach = q * jax.nn.sigmoid(q) * jnp.exp(range_sums(upto_ref[...], log_decay))
    decay = jnp.exp(jnp.sum(log_decay, axis=0, keepdims=True))
    for h in range(q_ref.shape[1] // HEAD):
        at = head_slice(h)
        o, du = o_ref[:, at], du_ref[:, at]
        size = lax.rsqrt(jnp.mean(o * o, axis=1, keepdims=True) + epsilon)
        normed = o * size
        dscale_ref[:, at] += jnp.sum(du * normed, axis=0, keepdims=True)
        scaled = du * scale_ref[:, at]
        do = size * (scaled - normed * jnp.mean(scaled * normed, axis=1, keepdims=True))
        do_ref[:, at] = do
        pack_store(out_ref, h, dot3(split(do), split(reach[:, at]), 0, 0), decay[:, at])


def back_inside_kernel(levels_ref, fb_ref, q_ref, f_ref, i_ref, do_ref, high_ref, low_ref, *refs):
    dq_ref, dk_ref, di_ref = refs[-3:]
    size = q_ref.shape[0]
    count = levels_ref.shape[0] // size
    z = f_ref[...] + fb_ref[...]
    weights = jnp.exp(range_sums(levels_ref[...], log_decay_of(z)))
    keys = jax.nn.sigmoid(-z)
    q = q_ref[...]
    query = q * jax.nn.sigmoid(q)
    row, col, differ = level_masks(size)
    for h in range(q_ref.shape[1] // HEAD):
        at = head_slice(h)
        hq, hk = query[:, at], keys[:, at]
        value, do = i_ref[:, at], do_ref[:, at]
        value2, do2 = split(value), split(do)
        di_ref[:, at] = dot3((high_ref[0, h], low_ref[0, h]), do2, 0, 0)
        forth = dot3(do2, value2, 1, 1)
        back = dot3(value2, do2, 1, 1)
        diagonal = jnp.sum(do * value, axis=1, keepdims=True)
        dq, dk = diagonal * hk, diagonal * hq
        for l in range(count):
            w = weights[l * size : (l + 1) * size, at]
            here = (differ >> l) == 1
            forth2 = split(jnp.where(here & (row > col), forth, 0.0))
            back2 = split(jnp.where(here & (row < col), back, 0.0))
            dq += w * dot3_wide(forth2, split(hk * w))
            dk += w * dot3_wide(back2, split(hq * w))
        dq_ref[:, at] = dq
        dk_ref[:, at] = dk


def back_output_kernel(
    me_ref,
    upto_ref,
    after_ref,
    from_ref,
    fb_ref,
    q_ref,
    f_ref,
    i_ref,
    do_ref,
    dq_ref,
    dk_ref,
    di_ref,
    first_ref,
    end_ref,
    grad_ref,
    out_ref,
    again_ref,
    dbias_ref,
):
    @pl.when(pl.program_id(0) == 0)
    def _():
        dbias_ref[...] = jnp.zeros_like(dbias_ref)

    width = q_ref.shape[1]
    z = f_ref[...] + fb_ref[...]
    log_decay = log_decay_of(z)
    begin = jnp.exp(range_sums(upto_ref[...], log_decay))
    finish = jnp.exp(range_sums(after_ref[...], log_decay))
    keys = jax.nn.sigmoid(-z)
    q = q_ref[...]
    gate = jax.nn.sigmoid(q)
    query = q * gate
    for h in range(width // HEAD):
        at = head_slice(h)
        hk, hq = keys[:, at], query[:, at]
        grad = split(grad_ref[0, h])
        value, do = split(i_ref[:, at]), split(do_ref[:, at])
        dq = dq_ref[:, at] + begin[:, at] * dot3(do, split(first_ref[0, h]), 1, 0)
        dk = dk_ref[:, at] + finish[:, at] * dot3(value, grad, 1, 0)
        di = di_ref[:, at] + dot3(split(hk * finish[:, at]), grad, 1, 1)
        last = jnp.sum(grad_ref[0, h] * end_ref[0, h], axis=0, keepdims=True)
        dlog = range_sums(from_ref[...], hq * dq - hk * dk) + last
        dz = dlog * hk - dk * hk * (1.0 - hk)
        dbias_ref[:, at] += jnp.sum(dz, axis=0, keepdims=True)
        g = gate[:, at]
        out_ref[:, at] = (dq * (g * (1.0 + q[:, at] * (1.0 - g)))).astype(bf16)
        out_ref[:, slice(width + h * HEAD, width + (h + 1) * HEAD)] = dz.astype(bf16)
        out_ref[:, slice(2 * width + h * HEAD, 2 * width + (h + 1) * HEAD)] = di.astype(bf16)
    rows = out_ref.shape[0] // 2
    again_ref[0, 0, 0] = out_ref[:rows]
    again_ref[0, 1, 0] = out_ref[rows:]


def range_matrices(size):
    at = np.arange(size)
    row, col = at[:, None], at[None, :]
    upto = col <= row
    after = col > row
    since = col >= row
    levels = []
    for l in range(int(math.log2(size))):
        middle = (row >> (l + 1) << (l + 1)) + (1 << l)
        levels.append(np.where(row >= middle, (col >= middle) & (col <= row), (col > row) & (col < middle)))
    return [jnp.asarray(m, bf16) for m in (upto, after, since, np.concatenate(levels, axis=0))]


class Recurrence:
    def __init__(self, rows, width, size):
        self.size, self.width = size, width
        self.count, self.heads = rows // size, self.width // HEAD
        self.upto, self.after, self.since, self.levels = range_matrices(size)

    def whole(self, x):
        return pl.BlockSpec(x.shape, lambda s, *_: (0,) * x.ndim)

    def rows(self, column=0, wide=1, at=0):
        return pl.BlockSpec((self.size, self.width * wide), lambda s, *_: (s + at, column))

    def heads_spec(self, *tail, at=0):
        return pl.BlockSpec((1, self.heads) + tail, lambda s, *_: (s + at,) + (0,) * (1 + len(tail)))

    def rows_shape(self, dtype=f32, wide=1):
        return jax.ShapeDtypeStruct((self.count * self.size, self.width * wide), dtype)

    def heads_shape(self, *tail, dtype=f32):
        return jax.ShapeDtypeStruct((self.count, self.heads) + tail, dtype)

    def call(self, body, args, in_specs, out_specs, out_shape, name, us, prefetch=(), count=None, onto=None):
        aliases = None
        if onto is not None:
            aliases = {len(args) + k: k for k in range(len(onto))}
            args = args + tuple(onto)
            in_specs = in_specs + [pl.BlockSpec(memory_space=pl.ANY)] * len(onto)
        return kernel_call(
            body, (count or self.count,), in_specs, out_specs, out_shape, name, us, prefetch, aliases
        )(*prefetch, *args)

    def entry(self, x, pieces):
        d, wide = x.shape[1], 3 * self.width
        weight = jax.ShapeDtypeStruct((d, wide), bf16)
        last = jax.ShapeDtypeStruct((d, self.width), bf16)
        scales = jax.ShapeDtypeStruct((16, d), f32)
        row = pl.BlockSpec((self.size, d), lambda s, *_: (s, 0))
        one = jax.ShapeDtypeStruct((1, self.width), f32)
        outs = self.call(
            entry_kernel,
            (self.after, x) + tuple(pieces),
            [self.whole(self.after), row] + [self.whole(p) for p in pieces],
            [self.whole(scales), row, self.rows(0, 3), self.whole(weight), self.whole(last)]
            + [self.heads_spec(HEAD, HEAD), self.heads_spec(PACK, HEAD), self.whole(one)],
            [
                scales,
                jax.ShapeDtypeStruct(x.shape, bf16),
                self.rows_shape(f32, 3),
                weight,
                last,
                self.heads_shape(HEAD, HEAD),
                self.heads_shape(PACK, HEAD, dtype=bf16),
                one,
            ],
            "entry",
            17,
            (jnp.stack([lax.axis_index("fsdp"), lax.axis_index("rep")]).astype(jnp.int32),),
        )
        self.qfi, self.fb = outs[2], outs[7]
        return outs[:7]

    def inside(self, half, onto=None):
        x, fb, at = self.qfi, self.fb, half * (self.count // 2)
        square = self.heads_spec(self.size, self.size, at=at)
        return self.call(
            inside_kernel,
            (self.levels, fb, x, x, x),
            [self.whole(self.levels), self.whole(fb)] + [self.rows(k, at=at) for k in range(3)],
            [self.rows(at=at), square, square],
            [
                self.rows_shape(),
                self.heads_shape(self.size, self.size, dtype=bf16),
                self.heads_shape(self.size, self.size, dtype=bf16),
            ],
            "inside",
            15,
            count=self.count // 2,
            onto=onto,
        )

    def output(self, inside, first):
        x = self.qfi
        return self.call(
            output_kernel,
            (self.upto, self.fb, self.scale, x, x, inside, first),
            [self.whole(self.upto), self.whole(self.fb), self.whole(self.scale), self.rows(0), self.rows(1)]
            + [self.rows(), self.heads_spec(HEAD, HEAD)],
            [self.rows(), self.rows()],
            [self.rows_shape(), self.rows_shape(bf16)],
            "output",
            8,
        )

    def back_state(self, o, du):
        x = self.qfi
        row = jax.ShapeDtypeStruct((1, self.width), f32)
        return self.call(
            back_state_kernel,
            (self.upto, self.fb, self.scale, x, x, o, du),
            [self.whole(self.upto), self.whole(self.fb), self.whole(self.scale), self.rows(0), self.rows(1)]
            + [self.rows(), self.rows()],
            [self.rows(), self.heads_spec(PACK, HEAD), self.whole(row)],
            [self.rows_shape(), self.heads_shape(PACK, HEAD, dtype=bf16), row],
            "back_state",
            9,
        )

    def back_inside(self, do, high, low, half, onto=None):
        x, at = self.qfi, half * (self.count // 2)
        square = self.heads_spec(self.size, self.size, at=at)
        return self.call(
            back_inside_kernel,
            (self.levels, self.fb, x, x, x, do, high, low),
            [self.whole(self.levels), self.whole(self.fb)]
            + [self.rows(k, at=at) for k in range(3)]
            + [self.rows(at=at), square, square],
            [self.rows(at=at)] * 3,
            [self.rows_shape()] * 3,
            "back_inside",
            24,
            count=self.count // 2,
            onto=onto,
        )

    def back_output(self, do, dq, dk, di, first, end, grad):
        x = self.qfi
        row = jax.ShapeDtypeStruct((1, self.width), f32)
        state = self.heads_spec(HEAD, HEAD)
        half = self.count // 2

        def place(s, me):
            return (lax.rem(me[0] ^ s, 2), 0, (me[0] ^ s) // 2, 0, 0)

        return self.call(
            back_output_kernel,
            (self.upto, self.after, self.since, self.fb, x, x, x, do, dq, dk, di, first, end, grad),
            [self.whole(self.upto), self.whole(self.after), self.whole(self.since), self.whole(self.fb)]
            + [self.rows(0), self.rows(1), self.rows(2)]
            + [self.rows()] * 4
            + [state] * 3,
            [
                self.rows(0, 3),
                pl.BlockSpec((1, 2, 1, self.size // 2, self.width * 3), place),
                self.whole(row),
            ],
            [
                self.rows_shape(bf16, 3),
                jax.ShapeDtypeStruct((2, 2, half, self.size // 2, self.width * 3), bf16),
                row,
            ],
            "back_output",
            13,
            (index_of("rep"),),
        )


def parts_of(packed):
    wide = packed.astype(f32)
    return wide[:, :, :HEAD], wide[:, :, HEAD : HEAD + 1] + wide[:, :, HEAD + 16 : HEAD + 17]


def pack(state, decay):
    high, low = split(jnp.broadcast_to(decay, decay.shape[:2] + (16, HEAD)))
    return jnp.concatenate([state.astype(bf16), high, low], axis=2)


class Carry:
    def __init__(self, packed, reverse):
        self.reverse, self.shift, self.packed = reverse, 1, packed
        self.border, self.window = 0.0, 1.0
        self.send()

    def send(self):
        n, d = lax.axis_size("fsdp"), self.shift
        pairs = [(i, i - d) for i in range(d, n)] if self.reverse else [(i, i + d) for i in range(n - d)]
        self.flying = lax.ppermute(self.packed, "fsdp", pairs)
        self.sent = (self.packed,)

    def advance(self, *others):
        state, decay = parts_of(after(self.flying, *others))
        self.border = self.border + self.window * state
        self.window = self.window * decay
        self.shift *= 2
        self.flying = None
        if self.shift < lax.axis_size("fsdp"):
            own_state, own_decay = parts_of(self.packed)
            self.packed = pack(own_state + own_decay * state, own_decay * decay)
            self.send()

    def finish(self, *others):
        while self.flying is not None:
            self.advance(*others)
        return self.border


def nt(left, right):
    return lax.dot_general(left, right, (((1,), (1,)), ((), ())), preferred_element_type=f32)


def tn(left, right):
    return lax.dot_general(left, right, (((0,), (0,)), ((), ())), preferred_element_type=f32)


def middle_kernel(u_ref, weight_ref, x_ref, scale_ref, h_ref, b_ref):
    step, width = pl.program_id(0), weight_ref.shape[1]
    total = jnp.dot(u_ref[0], weight_ref[: u_ref.shape[2], :], preferred_element_type=f32)
    for r in range(1, u_ref.shape[0]):
        rows = slice(r * u_ref.shape[2], (r + 1) * u_ref.shape[2])
        total += jnp.dot(u_ref[r], weight_ref[rows, :], preferred_element_type=f32)
    at = pl.ds(pl.multiple_of(step * width, width), width)
    h_ref[:, at] = x_ref[:, at].astype(f32) + total

    @pl.when(step == pl.num_programs(0) - 1)
    def _():
        h = h_ref[...]
        size = lax.rsqrt(jnp.mean(h * h, axis=1, keepdims=True) + epsilon)
        b_ref[...] = (h * size * scale_ref[1:2, :]).astype(bf16)


def middle(u, weight, x, scales):
    rows, d = x.shape
    block = 512
    return kernel_call(
        middle_kernel,
        (d // block,),
        [whole_spec(u), pl.BlockSpec((d, block), lambda i: (0, i)), whole_spec(x), whole_spec(scales)],
        [whole_spec(x), whole_spec(x)],
        [jax.ShapeDtypeStruct(x.shape, f32), jax.ShapeDtypeStruct(x.shape, bf16)],
        "middle",
        6,
    )(u, weight, x, scales)


def back_middle_kernel(upper_ref, lower_ref, got_upper_ref, got_lower_ref, h_ref, dy_ref, scale_ref, weight_ref, *outs):
    dh_ref, dmo_ref, du_ref, dscale_ref = outs

    @pl.when(pl.program_id(0) == 0)
    def _():
        db = jnp.concatenate(
            [upper_ref[...] + got_upper_ref[...].astype(f32), lower_ref[...] + got_lower_ref[...].astype(f32)], axis=0
        )
        h = h_ref[...]
        size = lax.rsqrt(jnp.mean(h * h, axis=1, keepdims=True) + epsilon)
        normed = h * size
        dscale_ref[...] = jnp.sum(db * normed, axis=0, keepdims=True)
        scaled = db * scale_ref[1:2, :]
        dh = size * (scaled - normed * jnp.mean(scaled * normed, axis=1, keepdims=True)) + dy_ref[...].astype(f32)
        dh_ref[...] = dh
        dmo_ref[...] = dh.astype(bf16)

    total = nt(dmo_ref[...], weight_ref[...])
    width = du_ref.shape[2]
    for r in range(du_ref.shape[0]):
        du_ref[r] = total[:, r * width : (r + 1) * width]


def back_middle(parts, h, dy, scales, weight, width):
    rows, d = h.shape
    block = 512
    row = jax.ShapeDtypeStruct((1, d), f32)
    return kernel_call(
        back_middle_kernel,
        (d // block,),
        [whole_spec(x, 1) for x in parts]
        + [whole_spec(h, 1), whole_spec(dy, 1), whole_spec(scales), pl.BlockSpec((block, d), lambda i: (i, 0))],
        [whole_spec(h), whole_spec(dy), pl.BlockSpec((block // width, rows, width), lambda i: (i, 0, 0)), whole_spec(row)],
        [
            jax.ShapeDtypeStruct(h.shape, f32),
            jax.ShapeDtypeStruct(h.shape, bf16),
            jax.ShapeDtypeStruct((d // width, rows, width), f32),
            row,
        ],
        "back_middle",
        7,
    )(*parts, h, dy, scales, weight)


def joined(upper, lower, got_upper, got_lower):
    return jnp.concatenate([upper + got_upper.astype(f32), lower + got_lower.astype(f32)])


def feed_kernel(first, chunks, me_ref, b_ref, *refs):
    dy_refs, refs = refs[:chunks], refs[chunks:]
    if first:
        pieces_ref, down_ref, hidden_ref, gate_low_ref, up_low_ref, d_ref, gate_up_ref, rows_ref = refs

        @pl.when(pl.program_id(0) == 0)
        def _():
            width = pieces_ref.shape[3]
            for z in range(pieces_ref.shape[0]):
                gate_up_ref[:, :, z * width : (z + 1) * width] = pieces_ref[z]
            width = down_ref.shape[2]
            for r in range(down_ref.shape[0]):
                rows_ref[:, r * width : (r + 1) * width] = down_ref[r]
    else:
        gate_up_ref, rows_ref, hidden_ref, gate_low_ref, up_low_ref, d_ref, db_ref = refs
    d_ref[...] = jnp.concatenate([ref[...] for ref in dy_refs], axis=0)
    b = b_ref[...]
    gate = nt(b, gate_up_ref[0])
    up = nt(b, gate_up_ref[1])
    back = nt(d_ref[...], rows_ref[...])
    sigmoid = jax.nn.sigmoid(gate)
    silu = gate * sigmoid
    hidden_ref[...] = (silu * up).astype(bf16)
    gate_low_ref[...] = (back * up * (sigmoid * (1.0 + gate * (1.0 - sigmoid)))).astype(bf16)
    up_low_ref[...] = (back * silu).astype(bf16)
    if not first:
        total = jnp.dot(gate_low_ref[...], gate_up_ref[0], preferred_element_type=f32)
        total += jnp.dot(up_low_ref[...], gate_up_ref[1], preferred_element_type=f32)
        db_ref[...] = total.astype(bf16)


def feed(b, dy, weights, first):
    rows, d = b.shape
    ff = weights[-1].shape[-2]
    chips = lax.axis_size("rep") // 2
    half = dy.shape[0] // (4 * chips)
    chunks = 4

    def at(chunk):
        def block(i, me):
            q = chunks * i + chunk
            device = me[0] ^ (2 * lax.rem(q, chips) + (0 if first else 1))
            return (2 * device + q // chips, 0)

        return pl.BlockSpec((half, d), block)

    wide = pl.BlockSpec((chunks * half, d), lambda i, me: (i, 0))
    thin = pl.BlockSpec((chunks * half, ff), lambda i, me: (i, 0))
    outs, specs = [jax.ShapeDtypeStruct((rows, ff), bf16)] * 3 + [jax.ShapeDtypeStruct(b.shape, bf16)], [thin] * 3 + [wide]
    if first:
        whole = [jax.ShapeDtypeStruct((2, ff, d), bf16), jax.ShapeDtypeStruct((ff, d), bf16)]
        outs, specs = outs + whole, specs + [whole_spec(x) for x in whole]
    else:
        outs, specs = outs + [jax.ShapeDtypeStruct(b.shape, bf16)], specs + [wide]
    return kernel_call(
        functools.partial(feed_kernel, first, chunks),
        (rows // (chunks * half),),
        [wide] + [at(k) for k in range(chunks)] + [whole_spec(w, 1) for w in weights],
        specs,
        outs,
        "feed",
        20 if first else 27,
        (index_of("rep"),),
    )(index_of("rep"), b, *[dy] * chunks, *weights)


def source_kernel(count, turned, *refs):
    lefts, weights, refs = refs[: 4 * count], refs[4 * count : 5 * count], refs[5 * count :]
    got, outs = refs[:4], refs[4:]
    total = jnp.concatenate([ref[...] for ref in got], axis=0).astype(f32)
    for k in range(count):
        left = jnp.concatenate([ref[...] for ref in lefts[4 * k : 4 * k + 4]], axis=0)
        total += nt(left, weights[k][...]) if turned else jnp.dot(left, weights[k][...], preferred_element_type=f32)
    half = total.shape[0] // 2
    for q in range(2):

        @pl.when(pl.program_id(0) // (pl.num_programs(0) // 2) == q)
        def _(q=q):
            outs[2 * q][...] = total[:half].astype(outs[2 * q].dtype)
            outs[2 * q + 1][...] = total[half:].astype(outs[2 * q + 1].dtype)


def source(lefts, weights, got, rows, turned=False):
    chips = lax.axis_size("rep") // 2
    d = got.shape[1]
    steps = chips // 4

    def at(part):
        def block(s, *_):
            q, k = s // steps, 2 * lax.rem(s, steps) + part % 2
            upper = k + jnp.where(q == 0, chips // 2, 0)
            lower = chips + 2 * k + jnp.where(q == 0, 1, 0)
            return lower if part >= 2 else upper

        return block

    specs, args = [], []
    for left in lefts:
        for part in range(4):
            block = at(part)
            if left.ndim == 3:
                specs.append(pl.BlockSpec((None, rows, left.shape[2]), lambda s, block=block: (0, block(s), 0)))
            else:
                specs.append(pl.BlockSpec((rows, left.shape[1]), lambda s, block=block: (block(s), 0)))
            args.append(left)
    out = jax.ShapeDtypeStruct((chips // 2 * rows, d), bf16)
    kept = jax.ShapeDtypeStruct((chips // 2 * rows, d), f32)
    outs = kernel_call(
        functools.partial(source_kernel, len(lefts), turned),
        (2 * steps,),
        specs
        + [layer_spec(weights, k) for k in range(len(lefts))]
        + [pl.BlockSpec((rows, d), lambda s, block=at(part): (block(s), 0)) for part in range(4)],
        [pl.BlockSpec((2 * rows, d), lambda s, q=q: (jnp.clip(s - q * steps, 0, steps - 1), 0)) for q in (0, 0, 1, 1)],
        [out, out, kept, kept],
        "source",
        4 + 3 * len(lefts),
    )(*args, *[weights] * len(lefts), *[got] * 4)
    return [x.reshape(chips // 2, rows, d) for x in outs]


def grad_kernel(count, blocks, me_ref, *refs):
    lefts, rights, outs = refs[:count], refs[count : 2 * count], refs[2 * count :]
    total = tn(lefts[0][...], rights[0][...])
    for k in range(1, count):
        total += tn(lefts[k][...], rights[k][...])
    for j in range(blocks):

        @pl.when(pl.program_id(0) == blocks - 1 - j)
        def _(j=j):
            outs[j][...] = total.astype(outs[j].dtype)


def grad_blocks(lefts, rights, of_left):
    blocks = lax.axis_size("fsdp")

    def cut(x):
        width = x.shape[1] // blocks
        return pl.BlockSpec((x.shape[0], width), lambda s, me: (0, me[0] ^ (blocks - 1 - s)))

    specs = [cut(x) if of_left else whole_spec(x) for x in lefts]
    specs += [whole_spec(x) if of_left else cut(x) for x in rights]
    shape = (specs[0].block_shape[1], specs[-1].block_shape[1])
    return kernel_call(
        functools.partial(grad_kernel, len(lefts), blocks),
        (blocks,),
        specs,
        [pl.BlockSpec(shape, lambda s, me: (0, 0))] * blocks,
        [jax.ShapeDtypeStruct(shape, f32 if j == 0 else bf16) for j in range(blocks)],
        "grad",
        10,
        (index_of("fsdp"),),
    )(index_of("fsdp"), *lefts, *rights)


def grad_plain_kernel(count, *refs):
    total = tn(refs[0][...], refs[count][...])
    for k in range(1, count):
        total += tn(refs[k][...], refs[count + k][...])
    refs[-1][0] = total.astype(bf16)


def grad_plain(lefts, rights, width):
    rows, count = lefts[0].shape[1], rights[0].shape[1] // width
    return kernel_call(
        functools.partial(grad_plain_kernel, len(lefts)),
        (count,),
        [whole_spec(x) for x in lefts] + [pl.BlockSpec((x.shape[0], width), lambda s: (0, s)) for x in rights],
        pl.BlockSpec((1, rows, width), lambda s: (s, 0, 0)),
        jax.ShapeDtypeStruct((count, rows, width), bf16),
        "grad_plain",
        11,
    )(*lefts, *rights)


def grad_out_kernel(blocks, me_ref, u_ref, dmo_ref, *outs):
    total = jnp.concatenate([tn(u_ref[r], dmo_ref[...]) for r in range(u_ref.shape[0])], axis=0)
    for j in range(blocks):

        @pl.when(pl.program_id(0) == blocks - 1 - j)
        def _(j=j):
            outs[j][...] = total.astype(outs[j].dtype)


def grad_out_blocks(u, dmo):
    blocks = lax.axis_size("fsdp")
    each = u.shape[0] // blocks
    shape = (each * u.shape[2], dmo.shape[1])
    return kernel_call(
        functools.partial(grad_out_kernel, blocks),
        (blocks,),
        [pl.BlockSpec((each,) + u.shape[1:], lambda s, me: (me[0] ^ (blocks - 1 - s), 0, 0)), whole_spec(dmo)],
        [pl.BlockSpec(shape, lambda s, me: (0, 0))] * blocks,
        [jax.ShapeDtypeStruct(shape, f32 if j == 0 else bf16) for j in range(blocks)],
        "grad_out",
        6,
        (index_of("fsdp"),),
    )(index_of("fsdp"), u, dmo)


def rms_scale(value_input, scales):
    return (
        value_input
        * lax.rsqrt(jnp.mean(value_input * value_input, axis=-1, keepdims=True) + epsilon)
        * scales
    )


def product(left, right):
    return jnp.dot(left, right, preferred_element_type=f32)


def product_nt(left, right):
    return lax.dot_general(left, right, (((1,), (1,)), ((), ())), preferred_element_type=f32)


def adam(weight, first, second, gradient, step_rate, decay_on):
    first_new = beta_first * first + (1.0 - beta_first) * gradient
    second_new = beta_second * second + (1.0 - beta_second) * gradient * gradient
    first_fix = 1.0 - beta_first**STEP
    second_fix = 1.0 - beta_second**STEP
    weight_new = weight - step_rate * (
        first_new / first_fix / (jnp.sqrt(second_new / second_fix) + adam_epsilon)
        + decay_on * weight
    )
    return (weight_new, first_new, second_new)


def shards(
    tokens,
    cotangent,
    lengths,
    w_mix,
    w_in,
    w_down,
    gains,
    m_mix,
    m_in,
    m_down,
    m_gain,
    v_mix,
    v_in,
    v_down,
    v_gain,
):
    reps, planes = lax.axis_size("rep"), lax.axis_size("fsdp")
    rep, plane = lax.axis_index("rep"), lax.axis_index("fsdp")
    size = tokens.shape[1]
    width = w_mix.shape[2]
    rows = reps * size

    gain_rows = jnp.pad(gains.astype(bf16), ((0, 12), (0, 4 * width - gains.shape[1])))
    block = jnp.concatenate([w_mix[j].astype(bf16) for j in range(4)], axis=1)
    pieces = z_pieces(jnp.concatenate([block, gain_rows]))
    x_all = lax.all_gather(tokens[0], "rep", axis=0, tiled=True)
    turned = w_in.astype(bf16).transpose(0, 2, 1)
    position = plane * size + jnp.arange(size)
    valid = (position < lengths[0])[:, None]
    dy = jnp.where(valid, cotangent[0], jnp.zeros_like(cotangent[0]))
    dy_all = lax.all_gather(dy, "rep", axis=0, tiled=True)
    mixer = Recurrence(rows, width, size)
    pieces[-1] = after(pieces[-1], dy, turned)
    scales, a_all, qfi, qfi_cols, out_cols, local, packed = mixer.entry(x_all, pieces)
    mixer.scale = lax.dynamic_slice(scales, (2, rep * width), (1, width))
    ff = w_in.shape[2]
    carry = Carry(packed, False)
    part = mixer.inside(0)
    state_landed = carry.flying
    carry.advance(part[0])
    more_landed = carry.flying
    own_fb = mixer.fb
    mixer.fb = after(own_fb, carry.packed)
    inside, score_high, score_low = mixer.inside(1, part)
    mixer.fb = own_fb
    first = carry.finish(inside)
    end = local + parts_of(packed)[1] * first
    down_cols = lax.all_gather(after(w_down.astype(bf16), more_landed), "fsdp", axis=0, tiled=True)
    turned, dy_all = lax.optimization_barrier((after(turned, more_landed), dy_all))
    gate_up = lax.all_gather(turned, "fsdp", axis=0)
    o, u = mixer.output(after(inside, dy_all), first)
    u_got = rep_exchange(u.reshape(reps, size, width))
    out_full = place_columns(*rep_gather(after(out_cols, state_landed), lands=((more_landed, inside), (u_got,))))
    down_rows = rep_exchange(after(down_cols, u_got).reshape(reps, ff, width))
    h, b_own = middle(after(u_got, down_rows), out_full, tokens[0], scales)
    b_halves = rep_gather(b_own, before_far=(gate_up,))
    u_all = lax.all_gather(after(u, b_halves[1]), "rep", axis=0)

    b_halves = [half.reshape(rows // 2, D) for half in b_halves]
    hidden_near, gate_near, up_near, d_near, gate_up, down_rows = feed(b_halves[0], dy_all, (gate_up, down_rows), True)
    hidden_far, gate_far, up_far, d_far, db_far = feed(b_halves[1], dy_all, (gate_up, down_rows), False)
    db = RepReduce(db_far)
    gate_part = grad_plain([gate_near, gate_far], [after(b, db_far) for b in b_halves], D // planes)
    grad_gate = lax.psum_scatter(gate_part, "fsdp", scatter_dimension=0)
    db.begin(*source([after(gate_near, gate_part), up_near], gate_up, db.got, size // 2))
    up_part = grad_plain([up_near, up_far], [after(b, *db.sent) for b in b_halves], D // planes)
    db.advance(up_part)
    grad_up = lax.psum_scatter(after(up_part, *db.landed), "fsdp", scatter_dimension=0)
    mixed_far = product(after(hidden_far, *db.sent), down_rows).astype(bf16)
    mixed_sum = RepReduce(mixed_far)
    db_parts = db.finish(mixed_far, u_all)

    dh, dmo, du_own, grad_scale_two = back_middle(db_parts, h, dy, scales, out_full, width)
    du = rep_exchange(du_own).reshape(rows, width)
    down_part = grad_plain([after(hidden_near, du_own), hidden_far], [d_near, d_far], width)
    mixed_parts = source([after(hidden_near, down_part)], down_rows[None], mixed_sum.got, size // 2)
    do, back_packed, grad_scale_head = mixer.back_state(o, after(du, *mixed_parts))
    carry = Carry(back_packed, True)
    part = mixer.back_inside(do, score_high, score_low, 0)
    down_part = rep_exchange(after(down_part, back_packed))
    carry.advance(part[0])
    mixed_sum.begin(*lax.optimization_barrier((*mixed_parts, back_packed))[:4])
    dq, dk, di = mixer.back_inside(after(do, carry.packed, grad_gate), score_high, score_low, 1, part)
    down_part = after(down_part, dq).reshape(planes, -1, width)
    down_sum = ZReduce([block_of(down_part, plane ^ j) for j in range(planes)])
    grad_state = carry.finish(dq)
    grad_state = after(grad_state, grad_up, *mixed_sum.flying)
    dqfi, dqfi_again, grad_bias = mixer.back_output(do, dq, dk, di, first, end, grad_state)
    dqfi_again = dqfi_again.reshape(2, rows // 2, 3 * width)
    down_sum.advance(dqfi)
    qfi_sum = ZReduce(grad_blocks([a_all], [after(dqfi, *down_sum.landed)], True))
    again = after(dqfi_again, *qfi_sum.sent)
    da = RepReduce(product_nt(again[1], qfi_cols).astype(bf16))
    da.begin(*source([dqfi_again], qfi_cols[None], da.got, size // 2, True))
    gate_total, up_total = after(grad_gate, *da.sent).astype(f32), after(grad_up, *da.sent).astype(f32)
    dmo_cols = rep_exchange(after(dmo, *da.sent).reshape(size, reps, width).transpose(1, 0, 2)).reshape(rows, width)
    qfi_sum.advance(*da.sent)
    down_total = down_sum.finish(*da.sent)
    da.advance(*down_sum.landed)
    out_sum = ZReduce(grad_out_blocks(u_all, after(dmo_cols, *da.sent)))
    da_own = joined(*da.finish())
    grad_qfi_w = qfi_sum.finish(*da.landed)
    out_sum.advance(*da.landed)
    mixed_sum.advance(*da.landed)
    mixed = (h + joined(*mixed_sum.finish())).astype(bf16)
    norm_one, norm_one_pull = jax.vjp(rms_scale, tokens[0].astype(f32), scales[0])
    dx_norm, grad_scale_one = norm_one_pull(da_own)
    token_grad = dh + dx_norm
    grad_in = jnp.stack([gate_total, up_total]).transpose(0, 2, 1)
    grad_out_w = out_sum.finish()

    def spread(own):
        return lax.dynamic_update_slice_in_dim(jnp.zeros((1, D), f32), own, rep * width, 1)

    grad_gains = jnp.concatenate(
        [grad_scale_one[None], grad_scale_two, spread(grad_scale_head), spread(grad_bias)]
    )
    grad_gains = all_sum(after(all_sum(grad_gains, "rep"), *qfi_sum.landed), "fsdp")
    gain_owned = lax.dynamic_slice_in_dim(grad_gains, plane * gains.shape[1], gains.shape[1], 1)

    grad_mix = jnp.stack([grad_qfi_w[:, j * width : (j + 1) * width] for j in range(3)] + [grad_out_w])
    new_mix, first_mix, second_mix = adam(w_mix, m_mix, v_mix, grad_mix, rate_matrix, decay_matrix)
    new_in, first_in, second_in = adam(w_in, m_in, v_in, grad_in, rate_matrix, decay_matrix)
    new_down, first_down, second_down = adam(
        w_down, m_down, v_down, down_total, rate_matrix, decay_matrix
    )
    new_gains, first_gains, second_gains = adam(gains, m_gain, v_gain, gain_owned, rate_gain, 0.0)
    return (
        mixed[None],
        token_grad[None],
        new_mix,
        new_in,
        new_down,
        new_gains,
        first_mix,
        first_in,
        first_down,
        first_gains,
        second_mix,
        second_in,
        second_down,
        second_gains,
        new_mix.astype(bf16),
        new_in.astype(bf16),
        new_down.astype(bf16),
    )


def solution(mesh):
    rows = P("rep", "fsdp", None)
    stack = P(None, "fsdp", "rep")
    flat = P("fsdp", "rep")
    gain = P(None, "fsdp")
    weights = (stack, stack, flat, gain)
    return jax.shard_map(
        shards,
        mesh=mesh,
        in_specs=(rows, rows, P("rep")) + weights * 3,
        out_specs=(rows, rows) + weights * 3 + (stack, stack, flat),
        check_vma=False,
    )
```

```python
import functools
import math

import jax
import jax.numpy as jnp
import numpy as np
from jax import lax
from jax.experimental import pallas as pl
from jax.experimental.pallas import tpu as pltpu
from jax.sharding import PartitionSpec as P

D = 2048
HEAD = 128
STEP = 10
PACK = HEAD + 32

epsilon = 1e-06
adam_epsilon = 1e-08
beta_first = 0.5
beta_second = 0.5
rate_matrix = 0.04
rate_gain = 0.3
decay_matrix = 0.1
bf16 = jnp.bfloat16
f32 = jnp.float32


def swap(x, axis, d):
    n = lax.axis_size(axis)
    return lax.ppermute(x, axis, [(i, i ^ d) for i in range(n)])


def block_of(x, index):
    return lax.dynamic_index_in_dim(x, index, 0, False)


def low_bit(j):
    return j & -j


def z_pieces(x, *lands):
    n = lax.axis_size("fsdp")
    pieces, landed = {0: x}, ()
    for hop in range(1, n.bit_length()):
        now = [j for j in range(n) if j.bit_count() == hop]
        got = {j: swap(after(pieces[j & (j - 1)], *landed), "fsdp", low_bit(j)) for j in now}
        if hop <= len(lands):
            got = {j: after(piece, *lands[hop - 1]) for j, piece in got.items()}
        pieces.update(got)
        landed = tuple(got.values())
    return [pieces[j] for j in range(n)]


def kernel_call(body, grid, in_specs, out_specs, out_shape, name, us, prefetch=(), aliases=None):
    return pl.pallas_call(
        body,
        grid_spec=pltpu.PrefetchScalarGridSpec(
            num_scalar_prefetch=len(prefetch), grid=grid, in_specs=in_specs, out_specs=out_specs
        ),
        out_shape=out_shape,
        name=name,
        input_output_aliases=aliases or {},
        cost_estimate=pl.CostEstimate(flops=0, bytes_accessed=int(us * 5e4), transcendentals=0),
        compiler_params=pltpu.CompilerParams(
            dimension_semantics=("arbitrary",) * len(grid), vmem_limit_bytes=52 * 1024 * 1024
        ),
    )


def whole_spec(x, buffers=2):
    return pl.BlockSpec(x.shape, lambda *_: (0,) * x.ndim, pipeline_mode=pl.Buffered(buffers))


def layer_spec(x, at):
    return pl.BlockSpec((None,) + x.shape[1:], lambda *_: (at, 0, 0), pipeline_mode=pl.Buffered(1))


def index_of(axis):
    return lax.axis_index(axis).astype(jnp.int32).reshape(1)


class ZReduce:
    def __init__(self, sums):
        self.sums = list(sums)
        self.left = list(range(len(self.sums) - 1, 0, -1))
        self.flying = []
        self.send()

    def send(self, *others):
        most = max(j.bit_count() for j in self.left)
        now = [j for j in self.left if j.bit_count() == most]
        self.left = [j for j in self.left if j.bit_count() < most]
        self.sent = [after(self.sums[j].astype(bf16), *others) for j in now]
        self.flying += [(j, swap(x, "fsdp", low_bit(j))) for j, x in zip(now, self.sent)]

    def advance(self, *others):
        first = not self.left
        landed, self.flying = self.flying, []
        self.landed = [got for _, got in landed]
        for j, got in landed:
            got = after(got, *others)
            self.sums[j & (j - 1)] = self.sums[j & (j - 1)].astype(f32) + got.astype(f32)
        if not first:
            self.send(*self.landed, *others)
        return self.sums[0]

    def flying_now(self):
        return [got for _, got in self.flying]

    def finish(self, *others):
        while self.flying:
            total = self.advance(*others)
        return total


def after(x, *others):
    return lax.optimization_barrier((x,) + others)[0]


def chip_masks():
    masks = []
    while 2 << len(masks) < lax.axis_size("rep"):
        masks.append(2 << len(masks))
    return masks


def rep_gather(x, sends=(), lands=(), before_far=()):
    rows = x.shape[0] // 2
    masks = chip_masks()
    upper, lower = x[None, :rows], x[None, rows:]
    for step in range(len(masks)):
        if step < len(sends):
            upper, lower = after(upper, *sends[step]), after(lower, *sends[step])
        got = swap(upper, "rep", masks[step])
        other = swap(lower, "rep", masks[-1 - step])
        got, other = lax.optimization_barrier((got, other) + tuple(lands[step] if step < len(lands) else ()))[:2]
        upper = jnp.concatenate([upper, got])
        lower = jnp.stack([lower, other], axis=1).reshape((2 * lower.shape[0],) + lower.shape[1:])
    near = after(jnp.stack([upper, lower]), *before_far)
    return near, swap(near, "rep", 1)


class RepReduce:
    def __init__(self, far):
        self.got = swap(far, "rep", 1)
        self.masks = chip_masks()

    def begin(self, send_upper, send_lower, keep_upper, keep_lower):
        self.upper, self.lower = keep_upper, keep_lower
        self.sent = (send_upper, send_lower)
        self.fly(0)

    def fly(self, step):
        self.flying = (
            swap(self.sent[0], "rep", self.masks[-1 - step]),
            swap(self.sent[1], "rep", self.masks[step]),
        )

    def advance(self, *others):
        self.landed = self.flying
        upper, lower = lax.optimization_barrier(tuple(self.flying) + others)[:2]
        self.flying = None
        if self.upper.shape[0] == 1:
            self.last = (upper[0], lower[0])
            return
        half = self.upper.shape[0] // 2
        *sent, self.upper, self.lower = step_sums(self.upper, upper, self.lower, lower)
        self.sent = sent
        self.fly(len(self.masks) - half.bit_length())

    def finish(self, *others):
        while self.flying is not None:
            self.advance(*others)
        return self.upper[0], self.lower[0], *self.last


def step_kernel(keep_upper_ref, got_upper_ref, keep_lower_ref, got_lower_ref, *outs):
    half = keep_upper_ref.shape[0] // 2
    for i in range(half):
        upper = keep_upper_ref[i] + got_upper_ref[i].astype(f32)
        outs[2][i] = upper
        outs[0][i] = (keep_upper_ref[half + i] + got_upper_ref[half + i].astype(f32)).astype(bf16)
        outs[3][i] = keep_lower_ref[2 * i] + got_lower_ref[2 * i].astype(f32)
        outs[1][i] = (keep_lower_ref[2 * i + 1] + got_lower_ref[2 * i + 1].astype(f32)).astype(bf16)


def step_sums(keep_upper, got_upper, keep_lower, got_lower):
    count, rows, d = keep_upper.shape
    block = 32
    whole = pl.BlockSpec((count, block, d), lambda i: (0, i, 0))
    half = pl.BlockSpec((count // 2, block, d), lambda i: (0, i, 0))
    shape = (count // 2, rows, d)
    return kernel_call(
        step_kernel,
        (rows // block,),
        [whole] * 4,
        [half] * 4,
        [jax.ShapeDtypeStruct(shape, bf16)] * 2 + [jax.ShapeDtypeStruct(shape, f32)] * 2,
        "step_sums",
        3,
    )(keep_upper, got_upper, keep_lower, got_lower)


def place_kernel(me_ref, near_ref, far_ref, out_ref):
    rows = near_ref.shape[2]
    near = pl.program_id(0) < pl.num_programs(0) // 2
    out_ref[:rows] = jnp.where(near, near_ref[0, 0], far_ref[0, 0])
    out_ref[rows:] = jnp.where(near, near_ref[1, 0], far_ref[1, 0])


def place_columns(near, far):
    _, chips, rows, width = near.shape
    return kernel_call(
        place_kernel,
        (2 * chips,),
        [
            pl.BlockSpec((2, 1, rows, width), lambda p, me: (0, jnp.minimum(p, chips - 1), 0, 0)),
            pl.BlockSpec((2, 1, rows, width), lambda p, me: (0, jnp.maximum(p - chips, 0), 0, 0)),
        ],
        pl.BlockSpec((2 * rows, width), lambda p, me: (0, me[0] ^ (2 * lax.rem(p, chips) + p // chips))),
        jax.ShapeDtypeStruct((2 * rows, 2 * chips * width), near.dtype),
        "place_columns",
        7,
        (index_of("rep"),),
    )(index_of("rep"), near, far)


def rep_exchange(x):
    return lax.all_to_all(x, "rep", 0, 0)


def all_sum(x, axis):
    d = 1
    while d < lax.axis_size(axis):
        x = x + swap(x, axis, d)
        d *= 2
    return x


def split(x):
    high = x.astype(bf16)
    return high, (x - high.astype(f32)).astype(bf16)


def dot3(a, b, ca, cb):
    left = jnp.concatenate([a[0], a[0], a[1]], axis=ca)
    right = jnp.concatenate([b[0], b[1], b[0]], axis=cb)
    return lax.dot_general(left, right, (((ca,), (cb,)), ((), ())), preferred_element_type=f32)


def dot3_wide(a, b):
    both = jnp.dot(a[0], jnp.concatenate(b, axis=1), preferred_element_type=f32)
    return both[:, :HEAD] + both[:, HEAD:] + jnp.dot(a[1], b[0], preferred_element_type=f32)


def range_sums(matrix, x):
    width = x.shape[1]
    both = jnp.dot(matrix, jnp.concatenate(split(x), axis=1), preferred_element_type=f32)
    return both[:, :width] + both[:, width:]


def log_decay_of(z):
    return jnp.minimum(z, 0.0) - jnp.log1p(jnp.exp(-jnp.abs(z)))


def head_slice(h):
    return slice(h * HEAD, (h + 1) * HEAD)


def pack_store(ref, h, state, decay):
    ref[0, h, :HEAD, :] = state.astype(bf16)
    high, low = split(jnp.broadcast_to(decay, (16, HEAD)))
    ref[0, h, HEAD : HEAD + 16, :] = high
    ref[0, h, HEAD + 16 :, :] = low


def entry_kernel(me_ref, after_ref, x_ref, *refs):
    *pieces, scale_ref, a_ref, qfi_ref, weight_ref, last_ref, state_ref, out_ref, fb_ref = refs
    rows, wide = pieces[0].shape[0] - 16, weight_ref.shape[1]
    width = fb_ref.shape[1]

    @pl.when(pl.program_id(0) == 0)
    def _():
        for j, piece in enumerate(pieces):
            at = pl.ds(pl.multiple_of((me_ref[0] ^ j) * rows, rows), rows)
            weight_ref[at, :] = piece[:rows, :wide]
            last_ref[at, :] = piece[:rows, wide:]
            scale_ref[:, at] = piece[rows:, :rows].astype(f32)
        fb_ref[...] = scale_ref[3:4, pl.ds(pl.multiple_of(me_ref[1] * width, width), width)]

    x = x_ref[...].astype(f32)
    size = lax.rsqrt(jnp.mean(x * x, axis=1, keepdims=True) + epsilon)
    a_ref[...] = (x * size * scale_ref[0:1, :]).astype(bf16)
    qfi_ref[...] = jnp.dot(a_ref[...], weight_ref[...], preferred_element_type=f32)
    z = qfi_ref[:, width : 2 * width] + fb_ref[...]
    log_decay = log_decay_of(z)
    to_end = range_sums(after_ref[...], log_decay)
    keys = jax.nn.sigmoid(-z) * jnp.exp(to_end)
    decay = jnp.exp(jnp.sum(log_decay, axis=0, keepdims=True))
    for h in range(width // HEAD):
        at = head_slice(h)
        value = qfi_ref[:, 2 * width + h * HEAD : 2 * width + (h + 1) * HEAD]
        state = dot3(split(value), split(keys[:, at]), 0, 0)
        state_ref[0, h] = state
        pack_store(out_ref, h, state, decay[:, at])


def level_masks(size):
    row = lax.broadcasted_iota(jnp.int32, (size, size), 0)
    col = lax.broadcasted_iota(jnp.int32, (size, size), 1)
    return row, col, row ^ col


def inside_kernel(levels_ref, fb_ref, q_ref, f_ref, i_ref, *refs):
    out_ref, high_ref, low_ref = refs[-3:]
    size = q_ref.shape[0]
    count = levels_ref.shape[0] // size
    z = f_ref[...] + fb_ref[...]
    weights = jnp.exp(range_sums(levels_ref[...], log_decay_of(z)))
    keys = jax.nn.sigmoid(-z)
    q = q_ref[...]
    query = q * jax.nn.sigmoid(q)
    row, col, differ = level_masks(size)
    later = row > col
    for h in range(q_ref.shape[1] // HEAD):
        at = head_slice(h)
        hq, hk = query[:, at], keys[:, at]
        scores = jnp.where(row == col, jnp.sum(hq * hk, axis=1, keepdims=True), 0.0)
        for l in range(count):
            w = weights[l * size : (l + 1) * size, at]
            part = dot3(split(hq * w), split(hk * w), 1, 1)
            scores = jnp.where(later & ((differ >> l) == 1), part, scores)
        high, low = split(scores)
        high_ref[0, h] = high
        low_ref[0, h] = low
        out_ref[:, at] = dot3((high, low), split(i_ref[:, at]), 1, 0)


def output_kernel(upto_ref, fb_ref, scale_ref, q_ref, f_ref, inside_ref, state_ref, out_ref, u_ref):
    q = q_ref[...]
    reach = q * jax.nn.sigmoid(q) * jnp.exp(range_sums(upto_ref[...], log_decay_of(f_ref[...] + fb_ref[...])))
    for h in range(q_ref.shape[1] // HEAD):
        at = head_slice(h)
        o = inside_ref[:, at] + dot3(split(reach[:, at]), split(state_ref[0, h]), 1, 1)
        out_ref[:, at] = o
        size = lax.rsqrt(jnp.mean(o * o, axis=1, keepdims=True) + epsilon)
        u_ref[:, at] = (o * size * scale_ref[:, at]).astype(bf16)


def back_state_kernel(upto_ref, fb_ref, scale_ref, q_ref, f_ref, o_ref, du_ref, do_ref, out_ref, dscale_ref):
    @pl.when(pl.program_id(0) == 0)
    def _():
        dscale_ref[...] = jnp.zeros_like(dscale_ref)

    q = q_ref[...]
    log_decay = log_decay_of(f_ref[...] + fb_ref[...])
    reach = q * jax.nn.sigmoid(q) * jnp.exp(range_sums(upto_ref[...], log_decay))
    decay = jnp.exp(jnp.sum(log_decay, axis=0, keepdims=True))
    for h in range(q_ref.shape[1] // HEAD):
        at = head_slice(h)
        o, du = o_ref[:, at], du_ref[:, at]
        size = lax.rsqrt(jnp.mean(o * o, axis=1, keepdims=True) + epsilon)
        normed = o * size
        dscale_ref[:, at] += jnp.sum(du * normed, axis=0, keepdims=True)
        scaled = du * scale_ref[:, at]
        do = size * (scaled - normed * jnp.mean(scaled * normed, axis=1, keepdims=True))
        do_ref[:, at] = do
        pack_store(out_ref, h, dot3(split(do), split(reach[:, at]), 0, 0), decay[:, at])


def back_inside_kernel(levels_ref, fb_ref, q_ref, f_ref, i_ref, do_ref, high_ref, low_ref, *refs):
    dq_ref, dk_ref, di_ref = refs[-3:]
    size = q_ref.shape[0]
    count = levels_ref.shape[0] // size
    z = f_ref[...] + fb_ref[...]
    weights = jnp.exp(range_sums(levels_ref[...], log_decay_of(z)))
    keys = jax.nn.sigmoid(-z)
    q = q_ref[...]
    query = q * jax.nn.sigmoid(q)
    row, col, differ = level_masks(size)
    for h in range(q_ref.shape[1] // HEAD):
        at = head_slice(h)
        hq, hk = query[:, at], keys[:, at]
        value, do = i_ref[:, at], do_ref[:, at]
        value2, do2 = split(value), split(do)
        di_ref[:, at] = dot3((high_ref[0, h], low_ref[0, h]), do2, 0, 0)
        forth = dot3(do2, value2, 1, 1)
        back = dot3(value2, do2, 1, 1)
        diagonal = jnp.sum(do * value, axis=1, keepdims=True)
        dq, dk = diagonal * hk, diagonal * hq
        for l in range(count):
            w = weights[l * size : (l + 1) * size, at]
            here = (differ >> l) == 1
            forth2 = split(jnp.where(here & (row > col), forth, 0.0))
            back2 = split(jnp.where(here & (row < col), back, 0.0))
            dq += w * dot3_wide(forth2, split(hk * w))
            dk += w * dot3_wide(back2, split(hq * w))
        dq_ref[:, at] = dq
        dk_ref[:, at] = dk


def back_output_kernel(
    me_ref,
    upto_ref,
    after_ref,
    from_ref,
    fb_ref,
    q_ref,
    f_ref,
    i_ref,
    do_ref,
    dq_ref,
    dk_ref,
    di_ref,
    first_ref,
    end_ref,
    grad_ref,
    out_ref,
    again_ref,
    dbias_ref,
):
    @pl.when(pl.program_id(0) == 0)
    def _():
        dbias_ref[...] = jnp.zeros_like(dbias_ref)

    width = q_ref.shape[1]
    z = f_ref[...] + fb_ref[...]
    log_decay = log_decay_of(z)
    begin = jnp.exp(range_sums(upto_ref[...], log_decay))
    finish = jnp.exp(range_sums(after_ref[...], log_decay))
    keys = jax.nn.sigmoid(-z)
    q = q_ref[...]
    gate = jax.nn.sigmoid(q)
    query = q * gate
    for h in range(width // HEAD):
        at = head_slice(h)
        hk, hq = keys[:, at], query[:, at]
        grad = split(grad_ref[0, h])
        value, do = split(i_ref[:, at]), split(do_ref[:, at])
        dq = dq_ref[:, at] + begin[:, at] * dot3(do, split(first_ref[0, h]), 1, 0)
        dk = dk_ref[:, at] + finish[:, at] * dot3(value, grad, 1, 0)
        di = di_ref[:, at] + dot3(split(hk * finish[:, at]), grad, 1, 1)
        last = jnp.sum(grad_ref[0, h] * end_ref[0, h], axis=0, keepdims=True)
        dlog = range_sums(from_ref[...], hq * dq - hk * dk) + last
        dz = dlog * hk - dk * hk * (1.0 - hk)
        dbias_ref[:, at] += jnp.sum(dz, axis=0, keepdims=True)
        g = gate[:, at]
        out_ref[:, at] = (dq * (g * (1.0 + q[:, at] * (1.0 - g)))).astype(bf16)
        out_ref[:, slice(width + h * HEAD, width + (h + 1) * HEAD)] = dz.astype(bf16)
        out_ref[:, slice(2 * width + h * HEAD, 2 * width + (h + 1) * HEAD)] = di.astype(bf16)
    rows = out_ref.shape[0] // 2
    again_ref[0, 0, 0] = out_ref[:rows]
    again_ref[0, 1, 0] = out_ref[rows:]


def range_matrices(size):
    at = np.arange(size)
    row, col = at[:, None], at[None, :]
    upto = col <= row
    after = col > row
    since = col >= row
    levels = []
    for l in range(int(math.log2(size))):
        middle = (row >> (l + 1) << (l + 1)) + (1 << l)
        levels.append(np.where(row >= middle, (col >= middle) & (col <= row), (col > row) & (col < middle)))
    return [jnp.asarray(m, bf16) for m in (upto, after, since, np.concatenate(levels, axis=0))]


class Recurrence:
    def __init__(self, rows, width, size):
        self.size, self.width = size, width
        self.count, self.heads = rows // size, self.width // HEAD
        self.upto, self.after, self.since, self.levels = range_matrices(size)

    def whole(self, x):
        return pl.BlockSpec(x.shape, lambda s, *_: (0,) * x.ndim)

    def rows(self, column=0, wide=1, at=0):
        return pl.BlockSpec((self.size, self.width * wide), lambda s, *_: (s + at, column))

    def heads_spec(self, *tail, at=0):
        return pl.BlockSpec((1, self.heads) + tail, lambda s, *_: (s + at,) + (0,) * (1 + len(tail)))

    def rows_shape(self, dtype=f32, wide=1):
        return jax.ShapeDtypeStruct((self.count * self.size, self.width * wide), dtype)

    def heads_shape(self, *tail, dtype=f32):
        return jax.ShapeDtypeStruct((self.count, self.heads) + tail, dtype)

    def call(self, body, args, in_specs, out_specs, out_shape, name, us, prefetch=(), count=None, onto=None):
        aliases = None
        if onto is not None:
            aliases = {len(args) + k: k for k in range(len(onto))}
            args = args + tuple(onto)
            in_specs = in_specs + [pl.BlockSpec(memory_space=pl.ANY)] * len(onto)
        return kernel_call(
            body, (count or self.count,), in_specs, out_specs, out_shape, name, us, prefetch, aliases
        )(*prefetch, *args)

    def entry(self, x, pieces):
        d, wide = x.shape[1], 3 * self.width
        weight = jax.ShapeDtypeStruct((d, wide), bf16)
        last = jax.ShapeDtypeStruct((d, self.width), bf16)
        scales = jax.ShapeDtypeStruct((16, d), f32)
        row = pl.BlockSpec((self.size, d), lambda s, *_: (s, 0))
        one = jax.ShapeDtypeStruct((1, self.width), f32)
        outs = self.call(
            entry_kernel,
            (self.after, x) + tuple(pieces),
            [self.whole(self.after), row] + [self.whole(p) for p in pieces],
            [self.whole(scales), row, self.rows(0, 3), self.whole(weight), self.whole(last)]
            + [self.heads_spec(HEAD, HEAD), self.heads_spec(PACK, HEAD), self.whole(one)],
            [
                scales,
                jax.ShapeDtypeStruct(x.shape, bf16),
                self.rows_shape(f32, 3),
                weight,
                last,
                self.heads_shape(HEAD, HEAD),
                self.heads_shape(PACK, HEAD, dtype=bf16),
                one,
            ],
            "entry",
            17,
            (jnp.stack([lax.axis_index("fsdp"), lax.axis_index("rep")]).astype(jnp.int32),),
        )
        self.qfi, self.fb = outs[2], outs[7]
        return outs[:7]

    def inside(self, half, onto=None):
        x, fb, at = self.qfi, self.fb, half * (self.count // 2)
        square = self.heads_spec(self.size, self.size, at=at)
        return self.call(
            inside_kernel,
            (self.levels, fb, x, x, x),
            [self.whole(self.levels), self.whole(fb)] + [self.rows(k, at=at) for k in range(3)],
            [self.rows(at=at), square, square],
            [
                self.rows_shape(),
                self.heads_shape(self.size, self.size, dtype=bf16),
                self.heads_shape(self.size, self.size, dtype=bf16),
            ],
            "inside",
            15,
            count=self.count // 2,
            onto=onto,
        )

    def output(self, inside, first):
        x = self.qfi
        return self.call(
            output_kernel,
            (self.upto, self.fb, self.scale, x, x, inside, first),
            [self.whole(self.upto), self.whole(self.fb), self.whole(self.scale), self.rows(0), self.rows(1)]
            + [self.rows(), self.heads_spec(HEAD, HEAD)],
            [self.rows(), self.rows()],
            [self.rows_shape(), self.rows_shape(bf16)],
            "output",
            8,
        )

    def back_state(self, o, du):
        x = self.qfi
        row = jax.ShapeDtypeStruct((1, self.width), f32)
        return self.call(
            back_state_kernel,
            (self.upto, self.fb, self.scale, x, x, o, du),
            [self.whole(self.upto), self.whole(self.fb), self.whole(self.scale), self.rows(0), self.rows(1)]
            + [self.rows(), self.rows()],
            [self.rows(), self.heads_spec(PACK, HEAD), self.whole(row)],
            [self.rows_shape(), self.heads_shape(PACK, HEAD, dtype=bf16), row],
            "back_state",
            9,
        )

    def back_inside(self, do, high, low, half, onto=None):
        x, at = self.qfi, half * (self.count // 2)
        square = self.heads_spec(self.size, self.size, at=at)
        return self.call(
            back_inside_kernel,
            (self.levels, self.fb, x, x, x, do, high, low),
            [self.whole(self.levels), self.whole(self.fb)]
            + [self.rows(k, at=at) for k in range(3)]
            + [self.rows(at=at), square, square],
            [self.rows(at=at)] * 3,
            [self.rows_shape()] * 3,
            "back_inside",
            24,
            count=self.count // 2,
            onto=onto,
        )

    def back_output(self, do, dq, dk, di, first, end, grad):
        x = self.qfi
        row = jax.ShapeDtypeStruct((1, self.width), f32)
        state = self.heads_spec(HEAD, HEAD)
        half = self.count // 2

        def place(s, me):
            return (lax.rem(me[0] ^ s, 2), 0, (me[0] ^ s) // 2, 0, 0)

        return self.call(
            back_output_kernel,
            (self.upto, self.after, self.since, self.fb, x, x, x, do, dq, dk, di, first, end, grad),
            [self.whole(self.upto), self.whole(self.after), self.whole(self.since), self.whole(self.fb)]
            + [self.rows(0), self.rows(1), self.rows(2)]
            + [self.rows()] * 4
            + [state] * 3,
            [
                self.rows(0, 3),
                pl.BlockSpec((1, 2, 1, self.size // 2, self.width * 3), place),
                self.whole(row),
            ],
            [
                self.rows_shape(bf16, 3),
                jax.ShapeDtypeStruct((2, 2, half, self.size // 2, self.width * 3), bf16),
                row,
            ],
            "back_output",
            13,
            (index_of("rep"),),
        )


def parts_of(packed):
    wide = packed.astype(f32)
    return wide[:, :, :HEAD], wide[:, :, HEAD : HEAD + 1] + wide[:, :, HEAD + 16 : HEAD + 17]


def pack(state, decay):
    high, low = split(jnp.broadcast_to(decay, decay.shape[:2] + (16, HEAD)))
    return jnp.concatenate([state.astype(bf16), high, low], axis=2)


class Carry:
    def __init__(self, packed, reverse):
        self.reverse, self.shift, self.packed = reverse, 1, packed
        self.border, self.window = 0.0, 1.0
        self.send()

    def send(self):
        n, d = lax.axis_size("fsdp"), self.shift
        pairs = [(i, i - d) for i in range(d, n)] if self.reverse else [(i, i + d) for i in range(n - d)]
        self.flying = lax.ppermute(self.packed, "fsdp", pairs)
        self.sent = (self.packed,)

    def advance(self, *others):
        state, decay = parts_of(after(self.flying, *others))
        self.border = self.border + self.window * state
        self.window = self.window * decay
        self.shift *= 2
        self.flying = None
        if self.shift < lax.axis_size("fsdp"):
            own_state, own_decay = parts_of(self.packed)
            self.packed = pack(own_state + own_decay * state, own_decay * decay)
            self.send()

    def finish(self, *others):
        while self.flying is not None:
            self.advance(*others)
        return self.border


def nt(left, right):
    return lax.dot_general(left, right, (((1,), (1,)), ((), ())), preferred_element_type=f32)


def tn(left, right):
    return lax.dot_general(left, right, (((0,), (0,)), ((), ())), preferred_element_type=f32)


def middle_kernel(u_ref, weight_ref, x_ref, scale_ref, h_ref, b_ref):
    step, width = pl.program_id(0), weight_ref.shape[1]
    total = jnp.dot(u_ref[0], weight_ref[: u_ref.shape[2], :], preferred_element_type=f32)
    for r in range(1, u_ref.shape[0]):
        rows = slice(r * u_ref.shape[2], (r + 1) * u_ref.shape[2])
        total += jnp.dot(u_ref[r], weight_ref[rows, :], preferred_element_type=f32)
    at = pl.ds(pl.multiple_of(step * width, width), width)
    h_ref[:, at] = x_ref[:, at].astype(f32) + total

    @pl.when(step == pl.num_programs(0) - 1)
    def _():
        h = h_ref[...]
        size = lax.rsqrt(jnp.mean(h * h, axis=1, keepdims=True) + epsilon)
        b_ref[...] = (h * size * scale_ref[1:2, :]).astype(bf16)


def middle(u, weight, x, scales):
    rows, d = x.shape
    block = 512
    return kernel_call(
        middle_kernel,
        (d // block,),
        [whole_spec(u), pl.BlockSpec((d, block), lambda i: (0, i)), whole_spec(x), whole_spec(scales)],
        [whole_spec(x), whole_spec(x)],
        [jax.ShapeDtypeStruct(x.shape, f32), jax.ShapeDtypeStruct(x.shape, bf16)],
        "middle",
        6,
    )(u, weight, x, scales)


def back_middle_kernel(upper_ref, lower_ref, got_upper_ref, got_lower_ref, h_ref, dy_ref, scale_ref, weight_ref, *outs):
    dh_ref, dmo_ref, du_ref, dscale_ref = outs

    @pl.when(pl.program_id(0) == 0)
    def _():
        db = jnp.concatenate(
            [upper_ref[...] + got_upper_ref[...].astype(f32), lower_ref[...] + got_lower_ref[...].astype(f32)], axis=0
        )
        h = h_ref[...]
        size = lax.rsqrt(jnp.mean(h * h, axis=1, keepdims=True) + epsilon)
        normed = h * size
        dscale_ref[...] = jnp.sum(db * normed, axis=0, keepdims=True)
        scaled = db * scale_ref[1:2, :]
        dh = size * (scaled - normed * jnp.mean(scaled * normed, axis=1, keepdims=True)) + dy_ref[...].astype(f32)
        dh_ref[...] = dh
        dmo_ref[...] = dh.astype(bf16)

    total = nt(dmo_ref[...], weight_ref[...])
    width = du_ref.shape[2]
    for r in range(du_ref.shape[0]):
        du_ref[r] = total[:, r * width : (r + 1) * width]


def back_middle(parts, h, dy, scales, weight, width):
    rows, d = h.shape
    block = 512
    row = jax.ShapeDtypeStruct((1, d), f32)
    return kernel_call(
        back_middle_kernel,
        (d // block,),
        [whole_spec(x, 1) for x in parts]
        + [whole_spec(h, 1), whole_spec(dy, 1), whole_spec(scales), pl.BlockSpec((block, d), lambda i: (i, 0))],
        [whole_spec(h), whole_spec(dy), pl.BlockSpec((block // width, rows, width), lambda i: (i, 0, 0)), whole_spec(row)],
        [
            jax.ShapeDtypeStruct(h.shape, f32),
            jax.ShapeDtypeStruct(h.shape, bf16),
            jax.ShapeDtypeStruct((d // width, rows, width), f32),
            row,
        ],
        "back_middle",
        7,
    )(*parts, h, dy, scales, weight)


def joined(upper, lower, got_upper, got_lower):
    return jnp.concatenate([upper + got_upper.astype(f32), lower + got_lower.astype(f32)])


def feed_kernel(first, chunks, me_ref, b_ref, *refs):
    dy_refs, refs = refs[:chunks], refs[chunks:]
    if first:
        pieces_ref, down_ref, hidden_ref, gate_low_ref, up_low_ref, d_ref, gate_up_ref, rows_ref = refs

        @pl.when(pl.program_id(0) == 0)
        def _():
            width = pieces_ref.shape[3]
            for z in range(pieces_ref.shape[0]):
                gate_up_ref[:, :, z * width : (z + 1) * width] = pieces_ref[z]
            width = down_ref.shape[2]
            for r in range(down_ref.shape[0]):
                rows_ref[:, r * width : (r + 1) * width] = down_ref[r]
    else:
        gate_up_ref, rows_ref, hidden_ref, gate_low_ref, up_low_ref, d_ref, db_ref = refs
    d_ref[...] = jnp.concatenate([ref[...] for ref in dy_refs], axis=0)
    b = b_ref[...]
    gate = nt(b, gate_up_ref[0])
    up = nt(b, gate_up_ref[1])
    back = nt(d_ref[...], rows_ref[...])
    sigmoid = jax.nn.sigmoid(gate)
    silu = gate * sigmoid
    hidden_ref[...] = (silu * up).astype(bf16)
    gate_low_ref[...] = (back * up * (sigmoid * (1.0 + gate * (1.0 - sigmoid)))).astype(bf16)
    up_low_ref[...] = (back * silu).astype(bf16)
    if not first:
        total = jnp.dot(gate_low_ref[...], gate_up_ref[0], preferred_element_type=f32)
        total += jnp.dot(up_low_ref[...], gate_up_ref[1], preferred_element_type=f32)
        db_ref[...] = total.astype(bf16)


def feed(b, dy, weights, first):
    rows, d = b.shape
    ff = weights[-1].shape[-2]
    chips = lax.axis_size("rep") // 2
    half = dy.shape[0] // (4 * chips)
    chunks = 4

    def at(chunk):
        def block(i, me):
            q = chunks * i + chunk
            device = me[0] ^ (2 * lax.rem(q, chips) + (0 if first else 1))
            return (2 * device + q // chips, 0)

        return pl.BlockSpec((half, d), block)

    wide = pl.BlockSpec((chunks * half, d), lambda i, me: (i, 0))
    thin = pl.BlockSpec((chunks * half, ff), lambda i, me: (i, 0))
    outs, specs = [jax.ShapeDtypeStruct((rows, ff), bf16)] * 3 + [jax.ShapeDtypeStruct(b.shape, bf16)], [thin] * 3 + [wide]
    if first:
        whole = [jax.ShapeDtypeStruct((2, ff, d), bf16), jax.ShapeDtypeStruct((ff, d), bf16)]
        outs, specs = outs + whole, specs + [whole_spec(x) for x in whole]
    else:
        outs, specs = outs + [jax.ShapeDtypeStruct(b.shape, bf16)], specs + [wide]
    return kernel_call(
        functools.partial(feed_kernel, first, chunks),
        (rows // (chunks * half),),
        [wide] + [at(k) for k in range(chunks)] + [whole_spec(w, 1) for w in weights],
        specs,
        outs,
        "feed",
        20 if first else 27,
        (index_of("rep"),),
    )(index_of("rep"), b, *[dy] * chunks, *weights)


def source_kernel(count, turned, *refs):
    lefts, weights, refs = refs[: 4 * count], refs[4 * count : 5 * count], refs[5 * count :]
    got, outs = refs[:4], refs[4:]
    total = jnp.concatenate([ref[...] for ref in got], axis=0).astype(f32)
    for k in range(count):
        left = jnp.concatenate([ref[...] for ref in lefts[4 * k : 4 * k + 4]], axis=0)
        total += nt(left, weights[k][...]) if turned else jnp.dot(left, weights[k][...], preferred_element_type=f32)
    half = total.shape[0] // 2
    for q in range(2):

        @pl.when(pl.program_id(0) // (pl.num_programs(0) // 2) == q)
        def _(q=q):
            outs[2 * q][...] = total[:half].astype(outs[2 * q].dtype)
            outs[2 * q + 1][...] = total[half:].astype(outs[2 * q + 1].dtype)


def source(lefts, weights, got, rows, turned=False):
    chips = lax.axis_size("rep") // 2
    d = got.shape[1]
    steps = chips // 4

    def at(part):
        def block(s, *_):
            q, k = s // steps, 2 * lax.rem(s, steps) + part % 2
            upper = k + jnp.where(q == 0, chips // 2, 0)
            lower = chips + 2 * k + jnp.where(q == 0, 1, 0)
            return lower if part >= 2 else upper

        return block

    specs, args = [], []
    for left in lefts:
        for part in range(4):
            block = at(part)
            if left.ndim == 3:
                specs.append(pl.BlockSpec((None, rows, left.shape[2]), lambda s, block=block: (0, block(s), 0)))
            else:
                specs.append(pl.BlockSpec((rows, left.shape[1]), lambda s, block=block: (block(s), 0)))
            args.append(left)
    out = jax.ShapeDtypeStruct((chips // 2 * rows, d), bf16)
    kept = jax.ShapeDtypeStruct((chips // 2 * rows, d), f32)
    outs = kernel_call(
        functools.partial(source_kernel, len(lefts), turned),
        (2 * steps,),
        specs
        + [layer_spec(weights, k) for k in range(len(lefts))]
        + [pl.BlockSpec((rows, d), lambda s, block=at(part): (block(s), 0)) for part in range(4)],
        [pl.BlockSpec((2 * rows, d), lambda s, q=q: (jnp.clip(s - q * steps, 0, steps - 1), 0)) for q in (0, 0, 1, 1)],
        [out, out, kept, kept],
        "source",
        4 + 3 * len(lefts),
    )(*args, *[weights] * len(lefts), *[got] * 4)
    return [x.reshape(chips // 2, rows, d) for x in outs]


def grad_kernel(count, blocks, me_ref, *refs):
    lefts, rights, outs = refs[:count], refs[count : 2 * count], refs[2 * count :]
    total = tn(lefts[0][...], rights[0][...])
    for k in range(1, count):
        total += tn(lefts[k][...], rights[k][...])
    for j in range(blocks):

        @pl.when(pl.program_id(0) == blocks - 1 - j)
        def _(j=j):
            outs[j][...] = total.astype(outs[j].dtype)


def grad_blocks(lefts, rights, of_left):
    blocks = lax.axis_size("fsdp")

    def cut(x):
        width = x.shape[1] // blocks
        return pl.BlockSpec((x.shape[0], width), lambda s, me: (0, me[0] ^ (blocks - 1 - s)))

    specs = [cut(x) if of_left else whole_spec(x) for x in lefts]
    specs += [whole_spec(x) if of_left else cut(x) for x in rights]
    shape = (specs[0].block_shape[1], specs[-1].block_shape[1])
    return kernel_call(
        functools.partial(grad_kernel, len(lefts), blocks),
        (blocks,),
        specs,
        [pl.BlockSpec(shape, lambda s, me: (0, 0))] * blocks,
        [jax.ShapeDtypeStruct(shape, f32 if j == 0 else bf16) for j in range(blocks)],
        "grad",
        10,
        (index_of("fsdp"),),
    )(index_of("fsdp"), *lefts, *rights)


def grad_plain_kernel(count, *refs):
    total = tn(refs[0][...], refs[count][...])
    for k in range(1, count):
        total += tn(refs[k][...], refs[count + k][...])
    refs[-1][0] = total.astype(bf16)


def grad_plain(lefts, rights, width):
    rows, count = lefts[0].shape[1], rights[0].shape[1] // width
    return kernel_call(
        functools.partial(grad_plain_kernel, len(lefts)),
        (count,),
        [whole_spec(x) for x in lefts] + [pl.BlockSpec((x.shape[0], width), lambda s: (0, s)) for x in rights],
        pl.BlockSpec((1, rows, width), lambda s: (s, 0, 0)),
        jax.ShapeDtypeStruct((count, rows, width), bf16),
        "grad_plain",
        11,
    )(*lefts, *rights)


def grad_out_kernel(blocks, me_ref, u_ref, dmo_ref, *outs):
    total = jnp.concatenate([tn(u_ref[r], dmo_ref[...]) for r in range(u_ref.shape[0])], axis=0)
    for j in range(blocks):

        @pl.when(pl.program_id(0) == blocks - 1 - j)
        def _(j=j):
            outs[j][...] = total.astype(outs[j].dtype)


def grad_out_blocks(u, dmo):
    blocks = lax.axis_size("fsdp")
    each = u.shape[0] // blocks
    shape = (each * u.shape[2], dmo.shape[1])
    return kernel_call(
        functools.partial(grad_out_kernel, blocks),
        (blocks,),
        [pl.BlockSpec((each,) + u.shape[1:], lambda s, me: (me[0] ^ (blocks - 1 - s), 0, 0)), whole_spec(dmo)],
        [pl.BlockSpec(shape, lambda s, me: (0, 0))] * blocks,
        [jax.ShapeDtypeStruct(shape, f32 if j == 0 else bf16) for j in range(blocks)],
        "grad_out",
        6,
        (index_of("fsdp"),),
    )(index_of("fsdp"), u, dmo)


def rms_scale(value_input, scales):
    return (
        value_input
        * lax.rsqrt(jnp.mean(value_input * value_input, axis=-1, keepdims=True) + epsilon)
        * scales
    )


def product(left, right):
    return jnp.dot(left, right, preferred_element_type=f32)


def product_nt(left, right):
    return lax.dot_general(left, right, (((1,), (1,)), ((), ())), preferred_element_type=f32)


def adam(weight, first, second, gradient, step_rate, decay_on):
    first_new = beta_first * first + (1.0 - beta_first) * gradient
    second_new = beta_second * second + (1.0 - beta_second) * gradient * gradient
    first_fix = 1.0 - beta_first**STEP
    second_fix = 1.0 - beta_second**STEP
    weight_new = weight - step_rate * (
        first_new / first_fix / (jnp.sqrt(second_new / second_fix) + adam_epsilon)
        + decay_on * weight
    )
    return (weight_new, first_new, second_new)


def shards(
    tokens,
    cotangent,
    lengths,
    w_mix,
    w_in,
    w_down,
    gains,
    m_mix,
    m_in,
    m_down,
    m_gain,
    v_mix,
    v_in,
    v_down,
    v_gain,
):
    reps, planes = lax.axis_size("rep"), lax.axis_size("fsdp")
    rep, plane = lax.axis_index("rep"), lax.axis_index("fsdp")
    size = tokens.shape[1]
    width = w_mix.shape[2]
    rows = reps * size

    gain_rows = jnp.pad(gains.astype(bf16), ((0, 12), (0, 4 * width - gains.shape[1])))
    block = jnp.concatenate([w_mix[j].astype(bf16) for j in range(4)], axis=1)
    pieces = z_pieces(jnp.concatenate([block, gain_rows]))
    x_all = lax.all_gather(tokens[0], "rep", axis=0, tiled=True)
    turned = w_in.astype(bf16).transpose(0, 2, 1)
    position = plane * size + jnp.arange(size)
    valid = (position < lengths[0])[:, None]
    dy = jnp.where(valid, cotangent[0], jnp.zeros_like(cotangent[0]))
    dy_all = lax.all_gather(dy, "rep", axis=0, tiled=True)
    mixer = Recurrence(rows, width, size)
    pieces[-1] = after(pieces[-1], dy, turned)
    scales, a_all, qfi, qfi_cols, out_cols, local, packed = mixer.entry(x_all, pieces)
    mixer.scale = lax.dynamic_slice(scales, (2, rep * width), (1, width))
    ff = w_in.shape[2]
    carry = Carry(packed, False)
    part = mixer.inside(0)
    state_landed = carry.flying
    carry.advance(part[0])
    more_landed = carry.flying
    own_fb = mixer.fb
    mixer.fb = after(own_fb, carry.packed)
    inside, score_high, score_low = mixer.inside(1, part)
    mixer.fb = own_fb
    first = carry.finish(inside)
    end = local + parts_of(packed)[1] * first
    down_cols = lax.all_gather(after(w_down.astype(bf16), more_landed), "fsdp", axis=0, tiled=True)
    turned, dy_all = lax.optimization_barrier((after(turned, more_landed), dy_all))
    gate_up = lax.all_gather(turned, "fsdp", axis=0)
    o, u = mixer.output(after(inside, dy_all), first)
    u_got = rep_exchange(u.reshape(reps, size, width))
    out_full = place_columns(*rep_gather(after(out_cols, state_landed), lands=((more_landed, inside), (u_got,))))
    down_rows = rep_exchange(after(down_cols, u_got).reshape(reps, ff, width))
    h, b_own = middle(after(u_got, down_rows), out_full, tokens[0], scales)
    b_halves = rep_gather(b_own, before_far=(gate_up,))
    u_all = lax.all_gather(after(u, b_halves[1]), "rep", axis=0)

    b_halves = [half.reshape(rows // 2, D) for half in b_halves]
    hidden_near, gate_near, up_near, d_near, gate_up, down_rows = feed(b_halves[0], dy_all, (gate_up, down_rows), True)
    hidden_far, gate_far, up_far, d_far, db_far = feed(b_halves[1], dy_all, (gate_up, down_rows), False)
    db = RepReduce(db_far)
    gate_part = grad_plain([gate_near, gate_far], [after(b, db_far) for b in b_halves], D // planes)
    grad_gate = lax.psum_scatter(gate_part, "fsdp", scatter_dimension=0)
    db.begin(*source([after(gate_near, gate_part), up_near], gate_up, db.got, size // 2))
    up_part = grad_plain([up_near, up_far], [after(b, *db.sent) for b in b_halves], D // planes)
    db.advance(up_part)
    grad_up = lax.psum_scatter(after(up_part, *db.landed), "fsdp", scatter_dimension=0)
    mixed_far = product(after(hidden_far, *db.sent), down_rows).astype(bf16)
    mixed_sum = RepReduce(mixed_far)
    db_parts = db.finish(mixed_far, u_all)

    dh, dmo, du_own, grad_scale_two = back_middle(db_parts, h, dy, scales, out_full, width)
    du = rep_exchange(du_own).reshape(rows, width)
    down_part = grad_plain([after(hidden_near, du_own), hidden_far], [d_near, d_far], width)
    mixed_parts = source([after(hidden_near, down_part)], down_rows[None], mixed_sum.got, size // 2)
    do, back_packed, grad_scale_head = mixer.back_state(o, after(du, *mixed_parts))
    carry = Carry(back_packed, True)
    part = mixer.back_inside(do, score_high, score_low, 0)
    down_part = rep_exchange(after(down_part, back_packed))
    carry.advance(part[0])
    mixed_sum.begin(*lax.optimization_barrier((*mixed_parts, back_packed))[:4])
    dq, dk, di = mixer.back_inside(after(do, carry.packed, grad_gate), score_high, score_low, 1, part)
    down_part = after(down_part, dq).reshape(planes, -1, width)
    down_sum = ZReduce([block_of(down_part, plane ^ j) for j in range(planes)])
    grad_state = carry.finish(dq)
    mixed_sum.advance(dq)
    grad_state = after(grad_state, grad_up, *mixed_sum.sent)
    dqfi, dqfi_again, grad_bias = mixer.back_output(do, dq, dk, di, first, end, grad_state)
    dqfi_again = dqfi_again.reshape(2, rows // 2, 3 * width)
    down_sum.advance(dqfi)
    qfi_sum = ZReduce(grad_blocks([a_all], [after(dqfi, *down_sum.landed, *mixed_sum.flying)], True))
    again = after(dqfi_again, *qfi_sum.sent)
    da = RepReduce(product_nt(again[1], qfi_cols).astype(bf16))
    da.begin(*source([dqfi_again], qfi_cols[None], da.got, size // 2, True))
    gate_total, up_total = after(grad_gate, *da.sent).astype(f32), after(grad_up, *da.sent).astype(f32)
    dmo_cols = rep_exchange(after(dmo, *da.sent).reshape(size, reps, width).transpose(1, 0, 2)).reshape(rows, width)
    qfi_sum.advance(*da.sent)
    down_total = down_sum.finish(*da.sent)
    da.advance(*down_sum.landed)
    out_sum = ZReduce(grad_out_blocks(u_all, after(dmo_cols, *da.sent)))
    da_own = joined(*da.finish())
    grad_qfi_w = qfi_sum.finish(*da.landed)
    out_sum.advance(*da.landed)
    mixed = (h + joined(*mixed_sum.finish(*da.landed))).astype(bf16)
    norm_one, norm_one_pull = jax.vjp(rms_scale, tokens[0].astype(f32), scales[0])
    dx_norm, grad_scale_one = norm_one_pull(da_own)
    token_grad = dh + dx_norm
    grad_in = jnp.stack([gate_total, up_total]).transpose(0, 2, 1)
    grad_out_w = out_sum.finish()

    def spread(own):
        return lax.dynamic_update_slice_in_dim(jnp.zeros((1, D), f32), own, rep * width, 1)

    grad_gains = jnp.concatenate(
        [grad_scale_one[None], grad_scale_two, spread(grad_scale_head), spread(grad_bias)]
    )
    grad_gains = all_sum(after(all_sum(grad_gains, "rep"), *qfi_sum.landed), "fsdp")
    gain_owned = lax.dynamic_slice_in_dim(grad_gains, plane * gains.shape[1], gains.shape[1], 1)

    grad_mix = jnp.stack([grad_qfi_w[:, j * width : (j + 1) * width] for j in range(3)] + [grad_out_w])
    new_mix, first_mix, second_mix = adam(w_mix, m_mix, v_mix, grad_mix, rate_matrix, decay_matrix)
    new_in, first_in, second_in = adam(w_in, m_in, v_in, grad_in, rate_matrix, decay_matrix)
    new_down, first_down, second_down = adam(
        w_down, m_down, v_down, down_total, rate_matrix, decay_matrix
    )
    new_gains, first_gains, second_gains = adam(gains, m_gain, v_gain, gain_owned, rate_gain, 0.0)
    return (
        mixed[None],
        token_grad[None],
        new_mix,
        new_in,
        new_down,
        new_gains,
        first_mix,
        first_in,
        first_down,
        first_gains,
        second_mix,
        second_in,
        second_down,
        second_gains,
        new_mix.astype(bf16),
        new_in.astype(bf16),
        new_down.astype(bf16),
    )


def solution(mesh):
    rows = P("rep", "fsdp", None)
    stack = P(None, "fsdp", "rep")
    flat = P("fsdp", "rep")
    gain = P(None, "fsdp")
    weights = (stack, stack, flat, gain)
    return jax.shard_map(
        shards,
        mesh=mesh,
        in_specs=(rows, rows, P("rep")) + weights * 3,
        out_specs=(rows, rows) + weights * 3 + (stack, stack, flat),
        check_vma=False,
    )
```
